256 devices in a mesh: pitch: 4 (over y), span: 4 (over x_hi, core), axial: 16 (over x_lo, z).
Axes of the slice: x: 4 (x_hi: 2, x_lo: 2; x = x_hi * 2 + x_lo), y: 4, z: 8, core: 2. Of those that a mesh axis runs over, the one named last changes fastest.
Arguments:
- state: float32 [5, 9, 16, 32, 2048], P(None, None, 'pitch', 'span', 'axial'), may hold values from -2 to 2
- source: float32 [5, 9, 16, 32, 2048], P(None, None, 'pitch', 'span', 'axial'), may hold values from -6 to 6
- velocity: float32 [3, 16, 32, 2048], P(None, 'pitch', 'span', 'axial'), may hold values from -4 to 4
- coupling: float32 [5, 5], replicated, may hold values from -2.5 to 2.5
- rotor: float32 [2], replicated, may hold values from 0.5 to 2.5
- face_map: int32 [32, 2048], P('span', 'axial'), may hold values from 0 to 1023, as said below
Outputs:
- smoothed: float32 [5, 9, 16, 32, 2048], P(None, None, 'pitch', 'span', 'axial')
The draws below stay inside these ranges and needn't reach their ends.
Inputs may be any that keep to these rules, and one draw needn't show every extreme that they name: `face_map`: within each aligned block of 8 hub-to-tip by 128 streamwise cells, the entries are a permutation of 0 to 1023.
All inputs are finite; a program needn't handle non-finite values.
Results may differ from the reference program's by a relative error of at most 0.0001.
Values sent between devices are 32-bit elements; how exact they have to be, the bound alone decides.
A program may use at most 128 MiB of HBM per device.

```python
import jax
import jax.numpy as jnp
from jax import lax

NVAR = 5
NT = 9
SWEEPS = 3
CS = 8
CA = 128
NP = 16
NS = 32
NA = 2048


def draw_face_map(key, part):
    key = jax.random.fold_in(key, 11)
    blocks_span = NS // CS
    blocks_axial = NA // CA
    keys = jax.random.split(key, blocks_span * blocks_axial)
    orders = jax.vmap(lambda single: jax.random.permutation(single, CS * CA))(keys)
    orders = orders.reshape(blocks_span, blocks_axial, CS, CA).transpose(0, 2, 1, 3).reshape(NS, NA)
    return orders.astype(jnp.int32)


def block_scale(rng, extent, cuts, least, largest):
    gain = 1.0
    for position, blocks in cuts:
        steps = jax.random.uniform(jax.random.fold_in(jax.random.fold_in(rng, 6), position), (blocks,), jnp.float32, least / len(cuts), largest / len(cuts))
        gain = gain * jnp.repeat(jnp.exp(steps), extent[position] // blocks).reshape((-1,) + (1,) * (len(extent) - 1 - position))
    return gain


def bell_draw(key, dims, scale, most, cuts=(), held_as=jnp.bfloat16):
    drawn = jax.random.normal(key, dims, jnp.float32) * scale
    if len(cuts) > 0:
        drawn = block_scale(key, dims, cuts, -0.22, 0.18) * drawn
    return jnp.clip(drawn, min=-most, max=most).astype(held_as)


def setup_inputs(seed: int = 0) -> dict:
    arg_keys = jax.random.split(jax.random.key(seed), 7)
    return {
        "state": bell_draw(arg_keys[0], (NVAR, NT, NP, NS, NA), 0.3, 2.0, ((2, 4), (3, 4), (4, 16)), jnp.float32),
        "source": bell_draw(arg_keys[1], (NVAR, NT, NP, NS, NA), 1.0, 6.0, ((2, 4), (3, 4), (4, 16)), jnp.float32),
        "velocity": bell_draw(arg_keys[2], (3, NP, NS, NA), 1.0, 4.0, ((1, 4), (2, 4), (3, 16)), jnp.float32),
        "coupling": bell_draw(arg_keys[3], (NVAR, NVAR), NVAR ** -0.5, 2.5, (), jnp.float32),
        "rotor": jnp.clip(jax.random.uniform(arg_keys[4], (2,), jnp.float32, 0.5, 2.5), 0.5, 2.5),
        "face_map": draw_face_map(jax.random.fold_in(arg_keys[6], 71), 0),
    }


VISCOSITY = 0.1
CFL_RATIO = 3.0
HIGHEST_PRECISION = lax.Precision.HIGHEST


def spectral_tables(rotor):
    frequency = rotor[0]
    lag_angle = rotor[1]
    instance = jnp.arange(NT, dtype=jnp.int32)
    offset = instance[:, None] - instance[None, :]
    offset_value = offset.astype(rotor.dtype)
    parity = (1 - 2 * (jnp.abs(offset) % 2)).astype(rotor.dtype)
    nonzero = jnp.where(offset == 0, jnp.ones_like(offset_value), offset_value)
    derivative = jnp.where(offset == 0, jnp.zeros_like(offset_value), 0.5 * parity / jnp.sin(jnp.pi * nonzero / NT))
    phase_step = 2.0 * jnp.pi * offset_value / NT
    harmonics = jnp.arange(1, (NT - 1) // 2 + 1, dtype=jnp.int32).astype(rotor.dtype)
    lead_map = (1.0 + 2.0 * jnp.sum(jnp.cos(harmonics[:, None, None] * (phase_step + lag_angle)[None]), axis=0)) / NT
    lag_map = (1.0 + 2.0 * jnp.sum(jnp.cos(harmonics[:, None, None] * (phase_step - lag_angle)[None]), axis=0)) / NT
    return frequency * derivative, lead_map, lag_map


def smoothing_coefficients(velocity):
    radius = jnp.abs(velocity) + 2.0 * VISCOSITY
    radius_sum = jnp.sum(radius, axis=0)
    ratio = CFL_RATIO * radius / radius_sum
    smoothing = 0.25 * jnp.maximum(ratio * ratio - 1.0, 0.0)
    diagonal = 1.0 + 2.0 * jnp.sum(smoothing, axis=0)
    return smoothing, diagonal


def neighbours(values, lead_map, lag_map, pair_rows, pair_cols):
    top_face = values[:, -1][:, pair_rows, pair_cols]
    lower_ghost = jnp.einsum("ij,jsa->isa", lead_map, top_face, precision=HIGHEST_PRECISION)
    shifted = jnp.einsum("ij,jsa->isa", lag_map, values[:, 0], precision=HIGHEST_PRECISION)
    upper_ghost = jnp.zeros_like(shifted).at[:, pair_rows, pair_cols].set(shifted)
    pitch_down = jnp.concatenate([lower_ghost[:, None], values[:, :-1]], axis=1)
    pitch_up = jnp.concatenate([values[:, 1:], upper_ghost[:, None]], axis=1)
    span_zero = jnp.zeros_like(values[:, :, :1])
    span_down = jnp.concatenate([span_zero, values[:, :, :-1]], axis=2)
    span_up = jnp.concatenate([values[:, :, 1:], span_zero], axis=2)
    axial_zero = jnp.zeros_like(values[:, :, :, :1])
    axial_down = jnp.concatenate([axial_zero, values[:, :, :, :-1]], axis=3)
    axial_up = jnp.concatenate([values[:, :, :, 1:], axial_zero], axis=3)
    return pitch_down, pitch_up, span_down, span_up, axial_down, axial_up


def reference(state, source, velocity, coupling, rotor, face_map):
    derivative, lead_map, lag_map = spectral_tables(rotor)
    smoothing, diagonal = smoothing_coefficients(velocity)
    span_index = jnp.arange(NS, dtype=jnp.int32)[:, None]
    axial_index = jnp.arange(NA, dtype=jnp.int32)[None, :]
    pair_rows = (span_index // CS) * CS + face_map // CA
    pair_cols = (axial_index // CA) * CA + face_map % CA

    def component(inputs):
        values, forcing, coupling_row = inputs
        beside_all = neighbours(values, lead_map, lag_map, pair_rows, pair_cols)
        coupled = jnp.tensordot(coupling_row, state, axes=1, precision=HIGHEST_PRECISION)
        time_term = jnp.einsum("ij,jpsa->ipsa", derivative, values, precision=HIGHEST_PRECISION)
        convect = jnp.zeros_like(values)
        for direction in range(3):
            speed = velocity[direction]
            convect = convect + jnp.maximum(speed, 0.0) * (values - beside_all[2 * direction]) + jnp.minimum(speed, 0.0) * (beside_all[2 * direction + 1] - values)
        total_around = beside_all[0] + beside_all[1] + beside_all[2] + beside_all[3] + beside_all[4] + beside_all[5]
        residual = forcing - time_term - coupled - convect + VISCOSITY * (total_around - 6.0 * values)
        result = residual
        for sweep_index in range(SWEEPS):
            cycle = neighbours(result, lead_map, lag_map, pair_rows, pair_cols)
            result = (residual + smoothing[0] * (cycle[0] + cycle[1]) + smoothing[1] * (cycle[2] + cycle[3]) + smoothing[2] * (cycle[4] + cycle[5])) / diagonal
        return result

    return lax.map(component, (state, source, coupling))
```

```python
import functools
import math

import jax
import jax.numpy as jnp
from jax import lax
from jax.experimental import pallas as pl
from jax.experimental.pallas import tpu as pltpu
from jax.sharding import PartitionSpec as P

NVAR = 5
NT = 9
PC = 4
CS = 8
CA = 128
ROWS = PC * CS
CELLS = (PC, CS, CA)
SWEEPS = 3
ROUNDS = SWEEPS + 1
VISCOSITY = 0.1
CFL_RATIO = 3.0
MESH = pl.DeviceIdType.MESH
HALF = (NT - 1) // 2


def roll(values, shift, axis):
    shift %= values.shape[axis]
    return values if shift == 0 else pltpu.roll(values, shift, axis)


def cells(rows):
    return rows.reshape(CELLS)


def flat(values):
    return values.reshape(ROWS, CA)


def kernel(
    state_ref, source_ref, velocity_ref, coupling_ref, rotor_ref, map_ref,
    out_ref,
    field, base, forcing, velocity, result, coef, weight, table, pick,
    pitch_ghost, span_send, span_ghost, axial_send, axial_ghost,
    load_sem, store_sem, send_sem, recv_sem,
):
    place = {a: lax.axis_index(a) for a in ("pitch", "span", "axial")}
    count = {a: lax.axis_size(a) for a in ("pitch", "span", "axial")}
    has_lower = {a: place[a] > 0 for a in ("span", "axial")}
    has_upper = {a: place[a] < count[a] - 1 for a in ("span", "axial")}
    pitch_up = lax.rem(place["pitch"] + 1, count["pitch"])
    pitch_down = lax.rem(place["pitch"] + count["pitch"] - 1, count["pitch"])
    on_first = place["pitch"] == 0
    on_last = place["pitch"] == count["pitch"] - 1

    barrier = pltpu.get_barrier_semaphore()
    for target in (pitch_up, pitch_down):
        pl.semaphore_signal(barrier, inc=1, device_id={"pitch": target}, device_id_type=MESH)
    for axis in ("span", "axial"):
        for there, step in ((has_lower[axis], -1), (has_upper[axis], 1)):

            @pl.when(there)
            def _():
                pl.semaphore_signal(
                    barrier, inc=1, device_id={axis: place[axis] + step}, device_id_type=MESH
                )

    loads = [
        pltpu.make_async_copy(state_ref, field.at[0], load_sem.at[0]),
        pltpu.make_async_copy(velocity_ref, velocity, load_sem.at[1]),
        pltpu.make_async_copy(source_ref, forcing, load_sem.at[2]),
    ]
    for load in loads:
        load.start()

    lane = lax.broadcasted_iota(jnp.int32, (PC, CS, CA), 2)
    row = lax.broadcasted_iota(jnp.int32, (CS, CA), 0)
    lane2 = lax.broadcasted_iota(jnp.int32, (CS, CA), 1)
    row4 = lax.broadcasted_iota(jnp.int32, (PC, CS, CA), 1)

    def transfers(k, v):
        source_of = state_ref if k == 0 else field.at[k]
        plan = (
            (None, None, source_of.at[v, :, pl.ds(ROWS - CS, CS)], pitch_ghost.at[k, 0, v], "pitch", pitch_up),
            (None, None, source_of.at[v, :, pl.ds(0, CS)], pitch_ghost.at[k, 1, v], "pitch", pitch_down),
            (has_upper["span"], has_lower["span"], span_send.at[k, 0, v], span_ghost.at[k, 0, v], "span", place["span"] + 1),
            (has_lower["span"], has_upper["span"], span_send.at[k, 1, v], span_ghost.at[k, 1, v], "span", place["span"] - 1),
            (has_upper["axial"], has_lower["axial"], axial_send.at[k, 0, v], axial_ghost.at[k, 0, v], "axial", place["axial"] + 1),
            (has_lower["axial"], has_upper["axial"], axial_send.at[k, 1, v], axial_ghost.at[k, 1, v], "axial", place["axial"] - 1),
        )
        for d, (sends, receives, src, dst, axis, target) in enumerate(plan):
            copy = pltpu.make_async_remote_copy(
                src_ref=src,
                dst_ref=dst,
                send_sem=send_sem.at[k, v, d],
                recv_sem=recv_sem.at[k, v, d],
                device_id={axis: target},
                device_id_type=MESH,
            )
            yield sends, receives, copy

    def guarded(condition, action):
        if condition is None:
            action()
        else:
            pl.when(condition)(action)

    def start(k, v):
        for sends, _, copy in transfers(k, v):
            guarded(sends, copy.start)

    def await_arrival(k, v):
        for _, receives, copy in transfers(k, v):
            guarded(receives, copy.wait_recv)

    def await_departure(k, v):
        for sends, _, copy in transfers(k, v):
            guarded(sends, copy.wait_send)

    def pack_axial(k, v, first, last):
        for d, packed in ((0, last), (1, first)):
            tile = packed[0]
            for p in range(1, PC):
                tile = jnp.where(lane2 >= 16 * p, roll(packed[p], 16 * p, 1), tile)
            axial_send[k, d, v] = tile

    def pack_span(k, v):
        for i in range(NT):
            at = pl.ds(i * PC, PC)
            span_send[k, 0, v, at, :] = field[k, v, i, pl.ds(CS - 1, PC, CS), :]
            span_send[k, 1, v, at, :] = field[k, v, i, pl.ds(0, PC, CS), :]

    def add_faces(values, i, packs):
        first, last = packs
        return (
            jnp.where(lane == i, roll(values, i, 2), first),
            jnp.where(lane == i, roll(values, i + 1, 2), last),
        )

    empty = jnp.zeros((PC, CS, CA), jnp.float32)

    for d, there in ((0, has_lower), (1, has_upper)):
        for axis, ghost in (("span", span_ghost), ("axial", axial_ghost)):

            @pl.when(jnp.logical_not(there[axis]))
            def _():
                def clear(v, carry):
                    for k in range(ROUNDS):
                        ghost[k, d, v] = jnp.zeros(ghost.shape[3:], jnp.float32)
                    return carry

                lax.fori_loop(0, NVAR, clear, 0)

    loads[0].wait()

    def pack_state(v, carry):
        packs = (empty, empty)
        for i in range(NT):
            packs = add_faces(cells(field[0, v, i]), i, packs)
        pack_axial(0, v, *packs)
        pack_span(0, v)
        return carry

    lax.fori_loop(0, NVAR, pack_state, 0)

    waits = 2 + sum(
        there[a].astype(jnp.int32) for there in (has_lower, has_upper) for a in ("span", "axial")
    )
    pl.semaphore_wait(barrier, waits)

    def send_state(v, carry):
        start(0, v)
        return carry

    lax.fori_loop(0, NVAR, send_state, 0)

    loads[1].wait()
    radius = [jnp.abs(velocity[d]) + 2.0 * VISCOSITY for d in range(3)]
    scale = CFL_RATIO / (radius[0] + radius[1] + radius[2])
    smoothing = []
    for d in range(3):
        ratio = radius[d] * scale
        smoothing.append(0.25 * jnp.maximum(ratio * ratio - 1.0, 0.0))
    inverse_diagonal = 1.0 / (1.0 + 2.0 * (smoothing[0] + smoothing[1] + smoothing[2]))
    centre = jnp.full((PC, CS, CA), -6.0 * VISCOSITY, jnp.float32)
    for d in range(3):
        weight[d] = smoothing[d] * inverse_diagonal
        speed = velocity[d]
        coef[2 * d] = jnp.maximum(speed, 0.0) + VISCOSITY
        coef[2 * d + 1] = VISCOSITY - jnp.minimum(speed, 0.0)
        centre = centre - jnp.abs(speed)
    weight[3] = inverse_diagonal
    coef[6] = centre

    frequency = rotor_ref[0]
    rates = [
        frequency * (0.5 * (1 - 2 * (n % 2)) / math.sin(math.pi * n / NT))
        for n in range(1, HALF + 1)
    ]
    loads[2].wait()

    def local_part(v, carry):
        x = [cells(field[0, v, i]) for i in range(NT)]
        own = coef[6]
        for i in range(NT):
            total = cells(forcing[v, i]) + own * x[i]
            for n in range(1, HALF + 1):
                total = total - rates[n - 1] * (x[(i - n) % NT] - x[(i + n) % NT])
            for w in range(NVAR):
                total = total - coupling_ref[v, w] * cells(field[0, w, i])
            field[1, v, i] = flat(total)
        return carry

    lax.fori_loop(0, NVAR, local_part, 0)

    @pl.when(jnp.logical_or(on_first, on_last))
    def _():
        angle = jnp.full((CS, CA), rotor_ref[1], jnp.float32)
        c1 = jnp.cos(angle)
        s1 = jnp.sin(angle) * jnp.where(on_first, 1.0, -1.0)
        c2, s2 = c1 * c1 - s1 * s1, 2.0 * s1 * c1
        c3, s3 = c2 * c1 - s2 * s1, s2 * c1 + c2 * s1
        c4, s4 = c2 * c2 - s2 * s2, 2.0 * s2 * c2
        for n in range(NT):
            total = jnp.full((CS, CA), 1.0 / NT, jnp.float32)
            for h, (c, s) in enumerate(((c1, s1), (c2, s2), (c3, s3), (c4, s4)), 1):
                theta = h * 2.0 * math.pi * n / NT
                total = total + (2.0 / NT * math.cos(theta)) * c - (2.0 / NT * math.sin(theta)) * s
            table[n] = total
        forward = map_ref[...]
        pick[0] = lax.shift_right_logical(forward, 7)
        pick[1] = lax.bitwise_and(forward, CA - 1)

    @pl.when(on_last)
    def _():
        rows, cols = pick[0], pick[1]
        column = lax.broadcasted_iota(jnp.int32, (CA, CA), 0)
        total = jnp.zeros((2 * CS, CA), jnp.float32)
        for s in range(CS):
            hit = rows[s : s + 1, :] == row
            left = jnp.concatenate(
                [
                    jnp.where(hit, float(s), 0.0),
                    jnp.where(hit, lane2.astype(jnp.float32), 0.0),
                ],
                axis=0,
            )
            right = jnp.where(cols[s : s + 1, :] == column, 1.0, 0.0)
            total = total + lax.dot_general(
                left, right, (((1,), (1,)), ((), ())), preferred_element_type=jnp.float32
            )
        pick[0] = total[:CS].astype(jnp.int32)
        pick[1] = total[CS:].astype(jnp.int32)

    def map_face(k, v):
        slot = jnp.where(on_first, 0, 1)

        @pl.when(jnp.logical_or(on_first, on_last))
        def _():
            rows, cols = pick[0], pick[1]
            picked = []
            for i in range(NT):
                total = jnp.zeros((CS, CA), jnp.float32)
                for s in range(CS):
                    line = pitch_ghost[k, slot, v, i, pl.ds(s, 1), :]
                    taken = jnp.take_along_axis(
                        jnp.broadcast_to(line, (CS, CA)), cols, axis=1, mode="promise_in_bounds"
                    )
                    total = jnp.where(rows == s, taken, total)
                picked.append(total)
            for i in range(NT):
                total = table[0] * picked[i]
                for n in range(1, NT):
                    total = total + table[n] * picked[(i - n) % NT]
                pitch_ghost[k, slot, v, i] = total

    def beside(k, v, i, axial):
        x = cells(field[k, v, i])
        pitch_low = jnp.concatenate([pitch_ghost[k, 0, v, i][None], x[: PC - 1]], axis=0)
        pitch_high = jnp.concatenate([x[1:], pitch_ghost[k, 1, v, i][None]], axis=0)
        lines = [
            jnp.stack(
                [
                    jnp.broadcast_to(span_ghost[k, d, v, pl.ds(i * PC + p, 1), :], (CS, CA))
                    for p in range(PC)
                ]
            )
            for d in range(2)
        ]
        span_low = jnp.where(row4 == 0, lines[0], roll(x, 1, 1))
        span_high = jnp.where(row4 == CS - 1, lines[1], roll(x, -1, 1))
        axial_low = jnp.where(lane == 0, roll(axial[0], -i, 2), roll(x, 1, 2))
        axial_high = jnp.where(lane == CA - 1, roll(axial[1], -i - 1, 2), roll(x, -1, 2))
        return pitch_low, pitch_high, span_low, span_high, axial_low, axial_high

    def unpack_axial(k, v):
        return [
            jnp.stack([roll(axial_ghost[k, d, v], -16 * p, 1) for p in range(PC)])
            for d in range(2)
        ]

    def residual_step(v, carry):
        await_departure(0, v)
        await_arrival(0, v)
        map_face(0, v)
        axial = unpack_axial(0, v)
        packs = (empty, empty)
        for i in range(NT):
            total = cells(field[1, v, i])
            for d, values in enumerate(beside(0, v, i, axial)):
                total = total + coef[d] * values
            field[1, v, i] = flat(total)
            base[v, i] = flat(total * weight[3])
            packs = add_faces(total, i, packs)
        pack_axial(1, v, *packs)
        pack_span(1, v)
        start(1, v)
        return carry

    lax.fori_loop(0, NVAR, residual_step, 0)

    def sweep_step(k, v, carry):
        last = k == ROUNDS - 1
        await_departure(k, v)
        await_arrival(k, v)
        map_face(k, v)
        axial = unpack_axial(k, v)
        packs = (empty, empty)
        for i in range(NT):
            near = beside(k, v, i, axial)
            total = cells(base[v, i])
            for d in range(3):
                total = total + weight[d] * (near[2 * d] + near[2 * d + 1])
            if last:
                result[v, i] = flat(total)
            else:
                field[k + 1, v, i] = flat(total)
                packs = add_faces(total, i, packs)
        if last:
            pltpu.make_async_copy(result.at[v], out_ref.at[v], store_sem.at[v]).start()
        else:
            pack_axial(k + 1, v, *packs)
            pack_span(k + 1, v)
            start(k + 1, v)
        return carry

    for k in range(1, ROUNDS):
        lax.fori_loop(0, NVAR, functools.partial(sweep_step, k), 0)

    def finish(v, carry):
        pltpu.make_async_copy(result.at[v], out_ref.at[v], store_sem.at[v]).wait()
        return carry

    lax.fori_loop(0, NVAR, finish, 0)


def per_device(state, source, velocity, coupling, rotor, face_map):
    block = (NVAR, NT, ROWS, CA)
    anywhere = pl.BlockSpec(memory_space=pl.ANY)
    scalars = pl.BlockSpec(memory_space=pltpu.SMEM)
    f32 = jnp.float32
    out = pl.pallas_call(
        kernel,
        out_shape=jax.ShapeDtypeStruct(block, f32),
        in_specs=[anywhere, anywhere, anywhere, scalars, scalars, pl.BlockSpec(memory_space=pltpu.VMEM)],
        out_specs=anywhere,
        scratch_shapes=[
            pltpu.VMEM((ROUNDS,) + block, f32),
            pltpu.VMEM(block, f32),
            pltpu.VMEM(block, f32),
            pltpu.VMEM((3, PC, CS, CA), f32),
            pltpu.VMEM(block, f32),
            pltpu.VMEM((7, PC, CS, CA), f32),
            pltpu.VMEM((4, PC, CS, CA), f32),
            pltpu.VMEM((NT, CS, CA), f32),
            pltpu.VMEM((2, CS, CA), jnp.int32),
            pltpu.VMEM((ROUNDS, 2, NVAR, NT, CS, CA), f32),
            pltpu.VMEM((ROUNDS, 2, NVAR, NT * PC, CA), f32),
            pltpu.VMEM((ROUNDS, 2, NVAR, NT * PC, CA), f32),
            pltpu.VMEM((ROUNDS, 2, NVAR, CS, CA), f32),
            pltpu.VMEM((ROUNDS, 2, NVAR, CS, CA), f32),
            pltpu.SemaphoreType.DMA((3,)),
            pltpu.SemaphoreType.DMA((NVAR,)),
            pltpu.SemaphoreType.DMA((ROUNDS, NVAR, 6)),
            pltpu.SemaphoreType.DMA((ROUNDS, NVAR, 6)),
        ],
        compiler_params=pltpu.CompilerParams(
            collective_id=0, has_side_effects=True, vmem_limit_bytes=32 * 1024 * 1024
        ),
        cost_estimate=pl.CostEstimate(flops=20_000_000, bytes_accessed=2_300_000, transcendentals=0),
    )(state.reshape(block), source.reshape(block), velocity, coupling, rotor, face_map)
    return out.reshape(state.shape)


def solution(mesh):
    return jax.shard_map(
        per_device,
        mesh=mesh,
        in_specs=(
            P(None, None, "pitch", "span", "axial"),
            P(None, None, "pitch", "span", "axial"),
            P(None, "pitch", "span", "axial"),
            P(),
            P(),
            P("span", "axial"),
        ),
        out_specs=P(None, None, "pitch", "span", "axial"),
        check_vma=False,
    )
```

```python
import functools
import math

import jax
import jax.numpy as jnp
from jax import lax
from jax.experimental import pallas as pl
from jax.experimental.pallas import tpu as pltpu
from jax.sharding import PartitionSpec as P

NVAR = 5
NT = 9
PC = 4
CS = 8
CA = 128
ROWS = PC * CS
CELLS = (PC, CS, CA)
SWEEPS = 3
ROUNDS = SWEEPS + 1
VISCOSITY = 0.1
CFL_RATIO = 3.0
MESH = pl.DeviceIdType.MESH
HALF = (NT - 1) // 2


def cells(rows):
    return rows.reshape(CELLS)


def flat(values):
    return values.reshape(ROWS, CA)


def kernel(
    state_ref, source_ref, velocity_ref, coupling_in, rotor_in, map_in,
    out_ref,
    field, partial, base, forcing, velocity, coef, weight, table, pick,
    beside_sum, shift, inject, mask,
    pitch_ghost, span_send, span_ghost, axial_send, axial_ghost,
    coupling_ref, rotor_ref, map_ref,
    load_sem, send_sem, recv_sem,
):
    place = {a: lax.axis_index(a) for a in ("pitch", "span", "axial")}
    count = {a: lax.axis_size(a) for a in ("pitch", "span", "axial")}
    has = {(a, 0): place[a] > 0 for a in ("span", "axial")}
    has.update({(a, 1): place[a] < count[a] - 1 for a in ("span", "axial")})
    both = {a: jnp.logical_and(has[a, 0], has[a, 1]) for a in ("span", "axial")}
    target = {(a, d): place[a] + 2 * d - 1 for a in ("span", "axial") for d in range(2)}
    target["pitch", 0] = lax.rem(place["pitch"] + count["pitch"] - 1, count["pitch"])
    target["pitch", 1] = lax.rem(place["pitch"] + 1, count["pitch"])
    on_first = place["pitch"] == 0
    on_last = place["pitch"] == count["pitch"] - 1

    def guarded(axis, d, action):
        if axis == "pitch":
            action()
        else:
            pl.when(has[axis, d])(action)

    barrier = pltpu.get_barrier_semaphore()
    for axis in ("pitch", "span", "axial"):
        for d in range(2):

            def greet():
                pl.semaphore_signal(
                    barrier, inc=1, device_id={axis: target[axis, d]}, device_id_type=MESH
                )

            guarded(axis, d, greet)

    loads = [
        pltpu.make_async_copy(src, dst, load_sem.at[n])
        for n, (src, dst) in enumerate(
            (
                (state_ref, field.at[0]),
                (velocity_ref, velocity),
                (source_ref, forcing),
                (coupling_in, coupling_ref),
                (rotor_in, rotor_ref),
                (map_in, map_ref),
            )
        )
    ]
    for load in loads:
        load.start()

    lane = lax.broadcasted_iota(jnp.int32, CELLS, 2)
    row = lax.broadcasted_iota(jnp.int32, (CS, CA), 0)
    lane2 = lax.broadcasted_iota(jnp.int32, (CS, CA), 1)
    row4 = lax.broadcasted_iota(jnp.int32, CELLS, 1)
    slot4 = lax.bitwise_and(lane, 63) - lax.broadcasted_iota(jnp.int32, CELLS, 0)

    def remote(src, dst, k, v, kind, axis, d):
        return pltpu.make_async_remote_copy(
            src_ref=src,
            dst_ref=dst,
            send_sem=send_sem.at[v, kind],
            recv_sem=recv_sem.at[k % 2, v, kind],
            device_id={axis: target[axis, d]},
            device_id_type=MESH,
        )

    def transfers(k, v, kind, axis, d):
        if axis == "pitch":
            faces = state_ref if k == 0 else field.at[k]
            src = faces.at[v, :, pl.ds((ROWS - CS) * d, CS)]
            ghost = pitch_ghost
        elif axis == "span":
            src, ghost = span_send.at[k, d, v], span_ghost
        else:
            src, ghost = axial_send.at[k, v], axial_ghost
        return remote(src, ghost.at[k, 1 - d, v], k, v, kind, axis, d)

    def start(k, v):
        for kind, axis in enumerate(("pitch", "span", "axial")):
            for d in range(2):
                guarded(axis, d, lambda: transfers(k, v, kind, axis, d).start())

    def await_pairs(k, v, arrival):
        for kind, (axis, ghost) in enumerate(
            (("pitch", pitch_ghost), ("span", span_ghost), ("axial", axial_ghost))
        ):

            def one(held, d):
                copy = remote(held, held, k, v, kind, axis, d)
                if arrival:
                    copy.wait_recv()
                else:
                    copy.wait_send()

            if axis == "pitch":
                one(ghost.at[k, :, v], 0)
            else:
                pl.when(both[axis])(lambda: one(ghost.at[k, :, v], 0))
                for d in range(2):
                    alone = jnp.logical_and(has[axis, d], jnp.logical_not(has[axis, 1 - d]))
                    pl.when(alone)(lambda: one(ghost.at[k, d, v], d))

    def pack_span(k, v):
        for i in range(NT):
            at = pl.ds(i * PC, PC)
            span_send[k, 0, v, at, :] = field[k, v, i, pl.ds(0, PC, CS), :]
            span_send[k, 1, v, at, :] = field[k, v, i, pl.ds(CS - 1, PC, CS), :]

    def split(values):
        high = values.astype(jnp.bfloat16)
        low = (values - high.astype(jnp.float32)).astype(jnp.bfloat16)
        return high, low

    def pack_axial(k, v, columns):
        tiles = columns.reshape(NT, PC, CS, CA)
        packed = tiles[0]
        for i in range(1, NT):
            packed = jnp.where(slot4 == i * PC, tiles[i], packed)
        tile = packed[0]
        for p in range(1, PC):
            tile = jnp.where(lax.bitwise_and(lane2, 3) == p, packed[p], tile)
        axial_send[k, v] = tile

    def shifted(k, v, columns):
        values = field[k, v].reshape(NT * ROWS, CA)
        return jnp.dot(
            jnp.concatenate(split(values), axis=1),
            shift[:, columns],
            preferred_element_type=jnp.float32,
        )

    for axis, ghost in (("span", span_ghost), ("axial", axial_ghost)):
        for d in range(2):

            @pl.when(jnp.logical_not(has[axis, d]))
            def _():
                def clear(v, carry):
                    for k in range(ROUNDS):
                        ghost[k, d, v] = jnp.zeros(ghost.shape[3:], jnp.float32)
                    return carry

                lax.fori_loop(0, NVAR, clear, 0)

    source_lane = lax.bitwise_and(lax.broadcasted_iota(jnp.int32, (2 * CA, 2 * CA), 0), CA - 1)
    result_lane = lax.broadcasted_iota(jnp.int32, (2 * CA, 2 * CA), 1)
    adjacent = jnp.abs(source_lane - result_lane) == 1
    spread = source_lane == jnp.where(result_lane < CA + 64, CA - 1, 0)
    shift[...] = jnp.where(
        result_lane < CA, jnp.where(adjacent, 1.0, 0.0), jnp.where(spread, 1.0, 0.0)
    ).astype(jnp.bfloat16)
    source_lane = source_lane[:, :CA]
    result_lane = result_lane[:, :CA]
    inject[...] = jnp.where(
        result_lane == jnp.where(source_lane < 64, 0, CA - 1), 1.0, 0.0
    ).astype(jnp.bfloat16)
    tile_of = lax.broadcasted_iota(jnp.int32, (NT * PC, CS, CA), 0)
    lane_of = lax.broadcasted_iota(jnp.int32, (NT * PC, CS, CA), 2)
    mask[...] = (
        jnp.where(tile_of == lax.bitwise_and(lane_of, 63), 1.0, 0.0)
        .reshape(NT * ROWS, CA)
        .astype(jnp.bfloat16)
        .reshape(NT * PC // 2, 2 * CS, CA)
    )

    loads[0].wait()

    def pack_state(v, carry):
        pack_axial(0, v, shifted(0, v, slice(CA, 2 * CA)))
        pack_span(0, v)
        return carry

    lax.fori_loop(0, NVAR, pack_state, 0)

    waits = 2 + sum(there.astype(jnp.int32) for there in has.values())
    pl.semaphore_wait(barrier, waits)

    def send_state(v, carry):
        start(0, v)
        return carry

    lax.fori_loop(0, NVAR, send_state, 0)

    loads[1].wait()
    radius = [jnp.abs(velocity[d]) + 2.0 * VISCOSITY for d in range(3)]
    scale = CFL_RATIO / (radius[0] + radius[1] + radius[2])
    smoothing = []
    for d in range(3):
        ratio = radius[d] * scale
        smoothing.append(0.25 * jnp.maximum(ratio * ratio - 1.0, 0.0))
    inverse_diagonal = 1.0 / (1.0 + 2.0 * (smoothing[0] + smoothing[1] + smoothing[2]))
    centre = jnp.full(CELLS, -6.0 * VISCOSITY, jnp.float32)
    lower, upper = [], []
    for d in range(3):
        speed = velocity[d]
        lower.append(jnp.maximum(speed, 0.0) + VISCOSITY)
        upper.append(VISCOSITY - jnp.minimum(speed, 0.0))
        centre = centre - jnp.abs(speed)
    smooth = [smoothing[d] * inverse_diagonal for d in range(3)]
    on_top, on_bottom = row4 == CS - 1, row4 == 0
    for held, low, high in ((coef, lower, upper), (weight, smooth, smooth)):
        held[0] = low[0]
        held[1] = high[0]
        held[2] = jnp.where(on_bottom, 0.0, low[1])
        held[3] = jnp.where(on_top, 0.0, high[1])
        held[4] = jnp.where(on_bottom, low[1], 0.0)
        held[5] = jnp.where(on_top, high[1], 0.0)
        held[6] = jnp.where(lane == 0, low[2], high[2])
    weight[7] = inverse_diagonal
    coef[7] = centre
    coef[8] = jnp.where(lane == 0, 0.0, lower[2])
    coef[9] = jnp.where(lane == CA - 1, 0.0, upper[2])

    for load in loads[2:]:
        load.wait()
    rates = [
        rotor_ref[0] * (0.5 * (1 - 2 * (n % 2)) / math.sin(math.pi * n / NT))
        for n in range(1, HALF + 1)
    ]

    zero = jnp.zeros((1, CS, CA), jnp.float32)

    def inside(held, x):
        below = jnp.concatenate([zero, x[: PC - 1]], axis=0)
        above = jnp.concatenate([x[1:], zero], axis=0)
        return (
            held[0] * below
            + held[1] * above
            + held[2] * pltpu.roll(x, 1, 1)
            + held[3] * pltpu.roll(x, CS - 1, 1)
        )

    def local_part(v, carry):
        x = [cells(field[0, v, i]) for i in range(NT)]
        for i in range(NT):
            total = cells(forcing[v, i]) + coef[7] * x[i] + inside(coef, x[i])
            total = total + coef[8] * pltpu.roll(x[i], 1, 2)
            total = total + coef[9] * pltpu.roll(x[i], CA - 1, 2)
            for n in range(1, HALF + 1):
                total = total - rates[n - 1] * (x[(i - n) % NT] - x[(i + n) % NT])
            for w in range(NVAR):
                total = total - coupling_ref[v, w] * cells(field[0, w, i])
            partial[v, i] = flat(total)
        return carry

    lax.fori_loop(0, NVAR, local_part, 0)

    @pl.when(jnp.logical_or(on_first, on_last))
    def _():
        angle = jnp.full((CS, CA), rotor_ref[1], jnp.float32)
        c1 = jnp.cos(angle)
        s1 = jnp.sin(angle) * jnp.where(on_first, 1.0, -1.0)
        c2, s2 = c1 * c1 - s1 * s1, 2.0 * s1 * c1
        c3, s3 = c2 * c1 - s2 * s1, s2 * c1 + c2 * s1
        c4, s4 = c2 * c2 - s2 * s2, 2.0 * s2 * c2
        for n in range(NT):
            total = jnp.full((CS, CA), 1.0 / NT, jnp.float32)
            for h, (c, s) in enumerate(((c1, s1), (c2, s2), (c3, s3), (c4, s4)), 1):
                theta = h * 2.0 * math.pi * n / NT
                total = total + (2.0 / NT * math.cos(theta)) * c - (2.0 / NT * math.sin(theta)) * s
            table[n] = total
        forward = map_ref[...]
        pick[0] = lax.shift_right_logical(forward, 7)
        pick[1] = lax.bitwise_and(forward, CA - 1)

    @pl.when(on_last)
    def _():
        rows, cols = pick[0], pick[1]
        column = lax.broadcasted_iota(jnp.int32, (CA, CA), 0)
        total = jnp.zeros((2 * CS, CA), jnp.float32)
        for s in range(CS):
            hit = rows[s : s + 1, :] == row
            left = jnp.concatenate(
                [
                    jnp.where(hit, float(s), 0.0),
                    jnp.where(hit, lane2.astype(jnp.float32), 0.0),
                ],
                axis=0,
            )
            right = jnp.where(cols[s : s + 1, :] == column, 1.0, 0.0)
            total = total + lax.dot_general(
                left, right, (((1,), (1,)), ((), ())), preferred_element_type=jnp.float32
            )
        pick[0] = total[:CS].astype(jnp.int32)
        pick[1] = total[CS:].astype(jnp.int32)

    def map_face(k, v):
        slot = jnp.where(on_first, 0, 1)

        @pl.when(jnp.logical_or(on_first, on_last))
        def _():
            rows, cols = pick[0], pick[1]
            picked = []
            for i in range(NT):
                total = jnp.zeros((CS, CA), jnp.float32)
                for s in range(CS):
                    line = pitch_ghost[k, slot, v, i, pl.ds(s, 1), :]
                    taken = jnp.take_along_axis(
                        jnp.broadcast_to(line, (CS, CA)), cols, axis=1, mode="promise_in_bounds"
                    )
                    total = jnp.where(rows == s, taken, total)
                picked.append(total)
            for i in range(NT):
                total = table[0] * picked[i]
                for n in range(1, NT):
                    total = total + table[n] * picked[(i - n) % NT]
                pitch_ghost[k, slot, v, i] = total

    def injected(k, v):
        tile = jnp.where(lane2 < 64, axial_ghost[k, 0, v], axial_ghost[k, 1, v])
        left = [
            (part[None] * mask[...]).reshape(NT * ROWS, CA)
            for part in split(jnp.concatenate([tile, tile], axis=0))
        ]
        ends = jnp.dot(
            jnp.concatenate(left, axis=1), inject[...], preferred_element_type=jnp.float32
        )
        return ends.reshape(NT, PC, CS, CA)

    def step(k, v, carry):
        held = coef if k == 0 else weight
        last = k == ROUNDS - 1
        await_pairs(k, v, True)
        map_face(k, v)
        ends = injected(k, v)
        for i in range(NT):
            faces = []
            for p in range(PC):
                at = pl.ds(i * PC + p, 1)
                face = held[4, p] * jnp.broadcast_to(span_ghost[k, 0, v, at, :], (CS, CA))
                face = face + held[5, p] * jnp.broadcast_to(span_ghost[k, 1, v, at, :], (CS, CA))
                if p == 0:
                    face = face + held[0, p] * pitch_ghost[k, 0, v, i]
                if p == PC - 1:
                    face = face + held[1, p] * pitch_ghost[k, 1, v, i]
                faces.append(face)
            total = cells(partial[v, i]) + held[6] * ends[i] + jnp.stack(faces)
            if k == 0:
                base[v, i] = flat(total * weight[7])
            if last:
                out_ref[v, i] = flat(total)
            else:
                field[k + 1, v, i] = flat(total)
        await_pairs(k, v, False)
        if last:
            return carry
        both_sides = shifted(k + 1, v, slice(0, 2 * CA))
        pack_axial(k + 1, v, both_sides[:, CA:])
        pack_span(k + 1, v)
        start(k + 1, v)
        beside_sum[...] = both_sides[:, :CA]
        for i in range(NT):
            x = cells(field[k + 1, v, i])
            around = cells(beside_sum[pl.ds(i * ROWS, ROWS), :])
            total = cells(base[v, i]) + inside(weight, x) + weight[6] * around
            partial[v, i] = flat(total)
        return carry

    for k in range(ROUNDS):
        lax.fori_loop(0, NVAR, functools.partial(step, k), 0)


def per_device(state, source, velocity, coupling, rotor, face_map):
    block = (NVAR, NT, ROWS, CA)
    anywhere = pl.BlockSpec(memory_space=pl.ANY)
    f32 = jnp.float32
    out = pl.pallas_call(
        kernel,
        out_shape=pltpu.VMEM(block, f32),
        in_specs=[anywhere] * 6,
        out_specs=pl.BlockSpec(memory_space=pltpu.VMEM),
        scratch_shapes=[
            pltpu.VMEM((ROUNDS,) + block, f32),
            pltpu.VMEM(block, f32),
            pltpu.VMEM(block, f32),
            pltpu.VMEM(block, f32),
            pltpu.VMEM((3,) + CELLS, f32),
            pltpu.VMEM((10,) + CELLS, f32),
            pltpu.VMEM((8,) + CELLS, f32),
            pltpu.VMEM((NT, CS, CA), f32),
            pltpu.VMEM((2, CS, CA), jnp.int32),
            pltpu.VMEM((NT * ROWS, CA), f32),
            pltpu.VMEM((2 * CA, 2 * CA), jnp.bfloat16),
            pltpu.VMEM((2 * CA, CA), jnp.bfloat16),
            pltpu.VMEM((NT * PC // 2, 2 * CS, CA), jnp.bfloat16),
            pltpu.VMEM((ROUNDS, 2, NVAR, NT, CS, CA), f32),
            pltpu.VMEM((ROUNDS, 2, NVAR, NT * PC, CA), f32),
            pltpu.VMEM((ROUNDS, 2, NVAR, NT * PC, CA), f32),
            pltpu.VMEM((ROUNDS, NVAR, CS, CA), f32),
            pltpu.VMEM((ROUNDS, 2, NVAR, CS, CA), f32),
            pltpu.SMEM((NVAR, NVAR), f32),
            pltpu.SMEM((2,), f32),
            pltpu.VMEM((CS, CA), jnp.int32),
            pltpu.SemaphoreType.DMA((6,)),
            pltpu.SemaphoreType.DMA((NVAR, 3)),
            pltpu.SemaphoreType.DMA((2, NVAR, 3)),
        ],
        compiler_params=pltpu.CompilerParams(
            collective_id=0, has_side_effects=True, vmem_limit_bytes=60 * 1024 * 1024
        ),
        cost_estimate=pl.CostEstimate(flops=20_000_000, bytes_accessed=2_300_000, transcendentals=0),
    )(state.reshape(block), source.reshape(block), velocity, coupling, rotor, face_map)
    return out.reshape(state.shape)


def solution(mesh):
    return jax.shard_map(
        per_device,
        mesh=mesh,
        in_specs=(
            P(None, None, "pitch", "span", "axial"),
            P(None, None, "pitch", "span", "axial"),
            P(None, "pitch", "span", "axial"),
            P(),
            P(),
            P("span", "axial"),
        ),
        out_specs=P(None, None, "pitch", "span", "axial"),
        check_vma=False,
    )
```

```python
import functools
import math

import jax
import jax.numpy as jnp
from jax import lax
from jax.experimental import pallas as pl
from jax.experimental.pallas import tpu as pltpu
from jax.sharding import PartitionSpec as P

NVAR = 5
NT = 9
PC = 4
CS = 8
CA = 128
ROWS = PC * CS
CELLS = (PC, CS, CA)
SWEEPS = 3
ROUNDS = SWEEPS + 1
VISCOSITY = 0.1
CFL_RATIO = 3.0
MESH = pl.DeviceIdType.MESH
HALF = (NT - 1) // 2


def cells(rows):
    return rows.reshape(CELLS)


def flat(values):
    return values.reshape(ROWS, CA)


def kernel(
    state_ref, source_ref, velocity_ref, coupling_in, rotor_in, map_in,
    out_ref,
    field, partial, base, forcing, velocity, coef, weight, table, pick,
    halves, shift, inject, mask,
    pitch_ghost, span_send, span_ghost, axial_send, axial_ghost,
    coupling_ref, rotor_ref, map_ref,
    load_sem, send_sem, recv_sem,
):
    place = {a: lax.axis_index(a) for a in ("pitch", "span", "axial")}
    count = {a: lax.axis_size(a) for a in ("pitch", "span", "axial")}
    axes = ("pitch", "span", "axial")
    has = {(a, 0): place[a] > 0 for a in axes[1:]}
    has.update({(a, 1): place[a] < count[a] - 1 for a in axes[1:]})
    both = {a: jnp.logical_and(has[a, 0], has[a, 1]) for a in axes[1:]}
    target = {(a, d): place[a] + 2 * d - 1 for a in axes[1:] for d in range(2)}
    target["pitch", 0] = lax.rem(place["pitch"] + count["pitch"] - 1, count["pitch"])
    target["pitch", 1] = lax.rem(place["pitch"] + 1, count["pitch"])
    on_first = place["pitch"] == 0
    on_last = place["pitch"] == count["pitch"] - 1

    def guarded(axis, d, action):
        if axis == "pitch":
            action()
        else:
            pl.when(has[axis, d])(action)

    barrier = pltpu.get_barrier_semaphore()
    for axis in axes:
        for d in range(2):

            def greet():
                pl.semaphore_signal(
                    barrier, inc=1, device_id={axis: target[axis, d]}, device_id_type=MESH
                )

            guarded(axis, d, greet)

    loads = [
        pltpu.make_async_copy(src, dst, load_sem.at[n])
        for n, (src, dst) in enumerate(
            (
                (state_ref, field.at[0]),
                (velocity_ref, velocity),
                (source_ref, forcing),
                (coupling_in, coupling_ref),
                (rotor_in, rotor_ref),
                (map_in, map_ref),
            )
        )
    ]
    for load in loads:
        load.start()

    lane = lax.broadcasted_iota(jnp.int32, CELLS, 2)
    row = lax.broadcasted_iota(jnp.int32, (CS, CA), 0)
    lane2 = lax.broadcasted_iota(jnp.int32, (CS, CA), 1)
    row4 = lax.broadcasted_iota(jnp.int32, CELLS, 1)
    slot4 = lax.bitwise_and(lane, 63) - lax.broadcasted_iota(jnp.int32, CELLS, 0)

    def remote(src, dst, k, v, kind, axis, d):
        return pltpu.make_async_remote_copy(
            src_ref=src,
            dst_ref=dst,
            send_sem=send_sem.at[v, kind],
            recv_sem=recv_sem.at[k % 2, v, kind],
            device_id={axis: target[axis, d]},
            device_id_type=MESH,
        )

    def transfers(k, v, kind, axis, d):
        if axis == "pitch":
            faces = state_ref if k == 0 else field.at[k]
            src = faces.at[v, :, pl.ds((ROWS - CS) * d, CS)]
            ghost = pitch_ghost
        elif axis == "span":
            src, ghost = span_send.at[k, d, v], span_ghost
        else:
            src, ghost = axial_send.at[k, v], axial_ghost
        return remote(src, ghost.at[k, 1 - d, v], k, v, kind, axis, d)

    def start(k, v, kind):
        axis = axes[kind]
        for d in range(2):
            guarded(axis, d, lambda: transfers(k, v, kind, axis, d).start())

    def await_pair(k, v, kind, arrival):
        axis, ghost = axes[kind], (pitch_ghost, span_ghost, axial_ghost)[kind]

        def one(held, d):
            copy = remote(held, held, k, v, kind, axis, d)
            if arrival:
                copy.wait_recv()
            else:
                copy.wait_send()

        if axis == "pitch":
            one(ghost.at[k, :, v], 0)
        else:
            pl.when(both[axis])(lambda: one(ghost.at[k, :, v], 0))
            for d in range(2):
                alone = jnp.logical_not(has[axis, 1 - d])
                pl.when(alone)(lambda: one(ghost.at[k, d, v], d))

    def pack_span(k, v):
        for i in range(NT):
            at = pl.ds(i * PC, PC)
            span_send[k, 0, v, at, :] = field[k, v, i, pl.ds(0, PC, CS), :]
            span_send[k, 1, v, at, :] = field[k, v, i, pl.ds(CS - 1, PC, CS), :]

    def split(values):
        high = values.astype(jnp.bfloat16)
        low = (values - high.astype(jnp.float32)).astype(jnp.bfloat16)
        return high, low

    def pack_axial(k, v, columns):
        tiles = columns.reshape(NT, PC, CS, CA)
        packed = tiles[0]
        for i in range(1, NT):
            packed = jnp.where(slot4 == i * PC, tiles[i], packed)
        tile = packed[0]
        for p in range(1, PC):
            tile = jnp.where(lax.bitwise_and(lane2, 3) == p, packed[p], tile)
        axial_send[k, v] = tile

    def shifted(k, v, columns):
        if columns.start:
            halves[...] = jnp.concatenate(split(field[k, v].reshape(NT * ROWS, CA)), axis=1)
        return jnp.dot(halves[...], shift[:, columns], preferred_element_type=jnp.float32)

    pl.semaphore_wait(barrier, 2 + sum(there.astype(jnp.int32) for there in has.values()))

    def send_faces(v, carry):
        start(0, v, 0)
        return carry

    lax.fori_loop(0, NVAR, send_faces, 0)

    source_lane = lax.bitwise_and(lax.broadcasted_iota(jnp.int32, (2 * CA, 2 * CA), 0), CA - 1)
    result_lane = lax.broadcasted_iota(jnp.int32, (2 * CA, 2 * CA), 1)
    adjacent = jnp.abs(source_lane - result_lane) == 1
    spread = source_lane == jnp.where(result_lane < CA + 64, CA - 1, 0)
    shift[...] = jnp.where(
        result_lane < CA, jnp.where(adjacent, 1.0, 0.0), jnp.where(spread, 1.0, 0.0)
    ).astype(jnp.bfloat16)
    source_lane = source_lane[:, :CA]
    result_lane = result_lane[:, :CA]
    inject[...] = jnp.where(
        result_lane == jnp.where(source_lane < 64, 0, CA - 1), 1.0, 0.0
    ).astype(jnp.bfloat16)
    tile_of = lax.broadcasted_iota(jnp.int32, (NT * PC, CS, CA), 0)
    lane_of = lax.broadcasted_iota(jnp.int32, (NT * PC, CS, CA), 2)
    mask[...] = (
        jnp.where(tile_of == lax.bitwise_and(lane_of, 63), 1.0, 0.0)
        .reshape(NT * ROWS, CA)
        .astype(jnp.bfloat16)
        .reshape(NT * PC // 2, 2 * CS, CA)
    )

    loads[0].wait()

    def pack_state(v, carry):
        pack_axial(0, v, shifted(0, v, slice(CA, 2 * CA)))
        start(0, v, 2)
        pack_span(0, v)
        start(0, v, 1)
        return carry

    lax.fori_loop(0, NVAR, pack_state, 0)

    for axis, ghost in (("span", span_ghost), ("axial", axial_ghost)):
        for d in range(2):

            @pl.when(jnp.logical_not(has[axis, d]))
            def _():
                def clear(v, carry):
                    for k in range(ROUNDS):
                        ghost[k, d, v] = jnp.zeros(ghost.shape[3:], jnp.float32)
                    return carry

                lax.fori_loop(0, NVAR, clear, 0)

    loads[1].wait()
    radius = [jnp.abs(velocity[d]) + 2.0 * VISCOSITY for d in range(3)]
    scale = CFL_RATIO / (radius[0] + radius[1] + radius[2])
    smoothing = []
    for d in range(3):
        ratio = radius[d] * scale
        smoothing.append(0.25 * jnp.maximum(ratio * ratio - 1.0, 0.0))
    inverse_diagonal = 1.0 / (1.0 + 2.0 * (smoothing[0] + smoothing[1] + smoothing[2]))
    centre = jnp.full(CELLS, -6.0 * VISCOSITY, jnp.float32)
    lower, upper = [], []
    for d in range(3):
        speed = velocity[d]
        lower.append(jnp.maximum(speed, 0.0) + VISCOSITY)
        upper.append(VISCOSITY - jnp.minimum(speed, 0.0))
        centre = centre - jnp.abs(speed)
    smooth = [smoothing[d] * inverse_diagonal for d in range(3)]
    on_top, on_bottom = row4 == CS - 1, row4 == 0
    for held, low, high in ((coef, lower, upper), (weight, smooth, smooth)):
        held[0] = low[0]
        held[1] = high[0]
        held[2] = jnp.where(on_bottom, 0.0, low[1])
        held[3] = jnp.where(on_top, 0.0, high[1])
        held[4] = jnp.where(on_bottom, low[1], 0.0)
        held[5] = jnp.where(on_top, high[1], 0.0)
        held[6] = jnp.where(lane == 0, low[2], high[2])
    weight[7] = inverse_diagonal
    weight[8] = smooth[2]
    coef[7] = centre
    coef[8] = jnp.where(lane == 0, 0.0, lower[2])
    coef[9] = jnp.where(lane == CA - 1, 0.0, upper[2])

    for load in loads[2:]:
        load.wait()
    rates = [
        rotor_ref[0] * (0.5 * (1 - 2 * (n % 2)) / math.sin(math.pi * n / NT))
        for n in range(1, HALF + 1)
    ]

    zero = jnp.zeros((1, CS, CA), jnp.float32)

    def inside(held, x):
        below = jnp.concatenate([zero, x[: PC - 1]], axis=0)
        above = jnp.concatenate([x[1:], zero], axis=0)
        return (
            held[0] * below
            + held[1] * above
            + held[2] * pltpu.roll(x, 1, 1)
            + held[3] * pltpu.roll(x, CS - 1, 1)
        )

    def local_part(v, carry):
        x = [cells(field[0, v, i]) for i in range(NT)]
        for i in range(NT):
            total = cells(forcing[v, i]) + coef[7] * x[i] + inside(coef, x[i])
            total = total + coef[8] * pltpu.roll(x[i], 1, 2)
            total = total + coef[9] * pltpu.roll(x[i], CA - 1, 2)
            for n in range(1, HALF + 1):
                total = total - rates[n - 1] * (x[(i - n) % NT] - x[(i + n) % NT])
            for w in range(NVAR):
                total = total - coupling_ref[v, w] * cells(field[0, w, i])
            partial[v, i] = flat(total)
        return carry

    lax.fori_loop(0, NVAR, local_part, 0)

    @pl.when(jnp.logical_or(on_first, on_last))
    def _():
        angle = jnp.full((CS, CA), rotor_ref[1], jnp.float32)
        c1 = jnp.cos(angle)
        s1 = jnp.sin(angle) * jnp.where(on_first, 1.0, -1.0)
        c2, s2 = c1 * c1 - s1 * s1, 2.0 * s1 * c1
        c3, s3 = c2 * c1 - s2 * s1, s2 * c1 + c2 * s1
        c4, s4 = c2 * c2 - s2 * s2, 2.0 * s2 * c2
        for n in range(NT):
            total = jnp.full((CS, CA), 1.0 / NT, jnp.float32)
            for h, (c, s) in enumerate(((c1, s1), (c2, s2), (c3, s3), (c4, s4)), 1):
                theta = h * 2.0 * math.pi * n / NT
                total = total + (2.0 / NT * math.cos(theta)) * c - (2.0 / NT * math.sin(theta)) * s
            table[n] = total
        forward = map_ref[...]
        pick[0] = lax.shift_right_logical(forward, 7)
        pick[1] = lax.bitwise_and(forward, CA - 1)

    @pl.when(on_last)
    def _():
        rows, cols = pick[0], pick[1]
        column = lax.broadcasted_iota(jnp.int32, (CA, CA), 0)
        total = jnp.zeros((2 * CS, CA), jnp.float32)
        for s in range(CS):
            hit = rows[s : s + 1, :] == row
            left = jnp.concatenate(
                [
                    jnp.where(hit, float(s), 0.0),
                    jnp.where(hit, lane2.astype(jnp.float32), 0.0),
                ],
                axis=0,
            )
            right = jnp.where(cols[s : s + 1, :] == column, 1.0, 0.0)
            total = total + lax.dot_general(
                left, right, (((1,), (1,)), ((), ())), preferred_element_type=jnp.float32
            )
        pick[0] = total[:CS].astype(jnp.int32)
        pick[1] = total[CS:].astype(jnp.int32)

    def map_face(k, v):
        slot = jnp.where(on_first, 0, 1)

        @pl.when(jnp.logical_or(on_first, on_last))
        def _():
            rows, cols = pick[0], pick[1]
            picked = []
            for i in range(NT):
                total = jnp.zeros((CS, CA), jnp.float32)
                for s in range(CS):
                    line = pitch_ghost[k, slot, v, i, pl.ds(s, 1), :]
                    taken = jnp.take_along_axis(
                        jnp.broadcast_to(line, (CS, CA)), cols, axis=1, mode="promise_in_bounds"
                    )
                    total = jnp.where(rows == s, taken, total)
                picked.append(total)
            for i in range(NT):
                total = table[0] * picked[i]
                for n in range(1, NT):
                    total = total + table[n] * picked[(i - n) % NT]
                pitch_ghost[k, slot, v, i] = total

    def injected(k, v):
        tile = jnp.where(lane2 < 64, axial_ghost[k, 0, v], axial_ghost[k, 1, v])
        left = [
            (part[None] * mask[...]).reshape(NT * ROWS, CA)
            for part in split(jnp.concatenate([tile, tile], axis=0))
        ]
        ends = jnp.dot(
            jnp.concatenate(left, axis=1), inject[...], preferred_element_type=jnp.float32
        )
        return ends.reshape(NT, PC, CS, CA)

    def step(k, v, carry):
        held = coef if k == 0 else weight
        last = k == ROUNDS - 1

        def complete(ends, i, p):
            at = pl.ds(i * PC + p, 1)
            rows = pl.ds(p * CS, CS)
            total = partial[v, i, rows] + held[6, p] * ends[i, p]
            total = total + held[4, p] * jnp.broadcast_to(span_ghost[k, 0, v, at, :], (CS, CA))
            total = total + held[5, p] * jnp.broadcast_to(span_ghost[k, 1, v, at, :], (CS, CA))
            if p == 0:
                total = total + held[0, p] * pitch_ghost[k, 0, v, i]
            if p == PC - 1:
                total = total + held[1, p] * pitch_ghost[k, 1, v, i]
            if k == 0:
                base[v, i, rows] = total * weight[7, p]
            if last:
                out_ref[v, i, rows] = total
            else:
                field[k + 1, v, i, rows] = total

        for kind in range(3):
            await_pair(k, v, kind, False)
        await_pair(k, v, 0, True)
        map_face(k, v)
        await_pair(k, v, 2, True)
        ends = injected(k, v)
        await_pair(k, v, 1, True)
        for i in range(NT):
            complete(ends, i, 0)
            complete(ends, i, PC - 1)
        if not last:
            start(k + 1, v, 0)
        for i in range(NT):
            for p in range(1, PC - 1):
                complete(ends, i, p)
        if last:
            return carry
        pack_axial(k + 1, v, shifted(k + 1, v, slice(CA, 2 * CA)))
        start(k + 1, v, 2)
        pack_span(k + 1, v)
        start(k + 1, v, 1)
        around = shifted(k + 1, v, slice(0, CA)).reshape(NT, PC, CS, CA)
        for i in range(NT):
            x = cells(field[k + 1, v, i])
            total = cells(base[v, i]) + inside(weight, x) + weight[8] * around[i]
            partial[v, i] = flat(total)
        return carry

    for k in range(ROUNDS):
        lax.fori_loop(0, NVAR, functools.partial(step, k), 0)


def per_device(state, source, velocity, coupling, rotor, face_map):
    block = (NVAR, NT, ROWS, CA)
    anywhere = pl.BlockSpec(memory_space=pl.ANY)
    f32 = jnp.float32
    out = pl.pallas_call(
        kernel,
        out_shape=pltpu.VMEM(block, f32),
        in_specs=[anywhere] * 6,
        out_specs=pl.BlockSpec(memory_space=pltpu.VMEM),
        scratch_shapes=[
            pltpu.VMEM((ROUNDS,) + block, f32),
            pltpu.VMEM(block, f32),
            pltpu.VMEM(block, f32),
            pltpu.VMEM(block, f32),
            pltpu.VMEM((3,) + CELLS, f32),
            pltpu.VMEM((10,) + CELLS, f32),
            pltpu.VMEM((9,) + CELLS, f32),
            pltpu.VMEM((NT, CS, CA), f32),
            pltpu.VMEM((2, CS, CA), jnp.int32),
            pltpu.VMEM((NT * ROWS, 2 * CA), jnp.bfloat16),
            pltpu.VMEM((2 * CA, 2 * CA), jnp.bfloat16),
            pltpu.VMEM((2 * CA, CA), jnp.bfloat16),
            pltpu.VMEM((NT * PC // 2, 2 * CS, CA), jnp.bfloat16),
            pltpu.VMEM((ROUNDS, 2, NVAR, NT, CS, CA), f32),
            pltpu.VMEM((ROUNDS, 2, NVAR, NT * PC, CA), f32),
            pltpu.VMEM((ROUNDS, 2, NVAR, NT * PC, CA), f32),
            pltpu.VMEM((ROUNDS, NVAR, CS, CA), f32),
            pltpu.VMEM((ROUNDS, 2, NVAR, CS, CA), f32),
            pltpu.SMEM((NVAR, NVAR), f32),
            pltpu.SMEM((2,), f32),
            pltpu.VMEM((CS, CA), jnp.int32),
            pltpu.SemaphoreType.DMA((6,)),
            pltpu.SemaphoreType.DMA((NVAR, 3)),
            pltpu.SemaphoreType.DMA((2, NVAR, 3)),
        ],
        compiler_params=pltpu.CompilerParams(
            collective_id=0, has_side_effects=True, vmem_limit_bytes=60 * 1024 * 1024
        ),
        cost_estimate=pl.CostEstimate(flops=20_000_000, bytes_accessed=2_300_000, transcendentals=0),
    )(state.reshape(block), source.reshape(block), velocity, coupling, rotor, face_map)
    return out.reshape(state.shape)


def solution(mesh):
    return jax.shard_map(
        per_device,
        mesh=mesh,
        in_specs=(
            P(None, None, "pitch", "span", "axial"),
            P(None, None, "pitch", "span", "axial"),
            P(None, "pitch", "span", "axial"),
            P(),
            P(),
            P("span", "axial"),
        ),
        out_specs=P(None, None, "pitch", "span", "axial"),
        check_vma=False,
    )
```

```python
import functools
import math

import jax
import jax.numpy as jnp
from jax import lax
from jax.experimental import pallas as pl
from jax.experimental.pallas import tpu as pltpu
from jax.sharding import PartitionSpec as P

NVAR = 5
NT = 9
PC = 4
CS = 8
CA = 128
ROWS = PC * CS
CELLS = (PC, CS, CA)
SWEEPS = 3
ROUNDS = SWEEPS + 1
VISCOSITY = 0.1
CFL_RATIO = 3.0
MESH = pl.DeviceIdType.MESH
HALF = (NT - 1) // 2


def cells(rows):
    return rows.reshape(CELLS)


def flat(values):
    return values.reshape(ROWS, CA)


def kernel(
    state_ref, source_ref, velocity_ref, coupling_in, rotor_in, map_in,
    out_ref,
    field, partial, base, forcing, velocity, coef, weight, table, pick,
    halves, shift, inject, mask,
    pitch_ghost, span_send, span_ghost, axial_send, axial_ghost,
    coupling_ref, rotor_ref, map_ref,
    load_sem, send_sem, recv_sem,
):
    place = {a: lax.axis_index(a) for a in ("pitch", "span", "axial")}
    count = {a: lax.axis_size(a) for a in ("pitch", "span", "axial")}
    axes = ("pitch", "span", "axial")
    has = {(a, 0): place[a] > 0 for a in axes[1:]}
    has.update({(a, 1): place[a] < count[a] - 1 for a in axes[1:]})
    both = {a: jnp.logical_and(has[a, 0], has[a, 1]) for a in axes[1:]}
    target = {(a, d): place[a] + 2 * d - 1 for a in axes[1:] for d in range(2)}
    target["pitch", 0] = lax.rem(place["pitch"] + count["pitch"] - 1, count["pitch"])
    target["pitch", 1] = lax.rem(place["pitch"] + 1, count["pitch"])
    on_first = place["pitch"] == 0
    on_last = place["pitch"] == count["pitch"] - 1

    def guarded(axis, d, action):
        if axis == "pitch":
            action()
        else:
            pl.when(has[axis, d])(action)

    barrier = pltpu.get_barrier_semaphore()
    for axis in axes:
        for d in range(2):

            def greet():
                pl.semaphore_signal(
                    barrier, inc=1, device_id={axis: target[axis, d]}, device_id_type=MESH
                )

            guarded(axis, d, greet)

    loads = [
        pltpu.make_async_copy(src, dst, load_sem.at[n])
        for n, (src, dst) in enumerate(
            (
                (state_ref, field.at[0]),
                (velocity_ref, velocity),
                (source_ref, forcing),
                (coupling_in, coupling_ref),
                (rotor_in, rotor_ref),
                (map_in, map_ref),
            )
        )
    ]
    for load in loads:
        load.start()

    lane = lax.broadcasted_iota(jnp.int32, CELLS, 2)
    row = lax.broadcasted_iota(jnp.int32, (CS, CA), 0)
    lane2 = lax.broadcasted_iota(jnp.int32, (CS, CA), 1)
    row4 = lax.broadcasted_iota(jnp.int32, CELLS, 1)
    slot4 = lax.bitwise_and(lane, 63) - lax.broadcasted_iota(jnp.int32, CELLS, 0)

    def remote(src, dst, k, v, kind, axis, d):
        return pltpu.make_async_remote_copy(
            src_ref=src,
            dst_ref=dst,
            send_sem=send_sem.at[v, kind],
            recv_sem=recv_sem.at[k % 2, v, kind],
            device_id={axis: target[axis, d]},
            device_id_type=MESH,
        )

    def transfers(k, v, kind, axis, d):
        if axis == "pitch":
            faces = state_ref if k == 0 else field.at[k]
            src = faces.at[v, :, pl.ds((ROWS - CS) * d, CS)]
            ghost = pitch_ghost
        elif axis == "span":
            src, ghost = span_send.at[k, d, v], span_ghost
        else:
            src, ghost = axial_send.at[k, v], axial_ghost
        return remote(src, ghost.at[k, 1 - d, v], k, v, kind, axis, d)

    def start(k, v, kind):
        axis = axes[kind]
        for d in range(2):
            guarded(axis, d, lambda: transfers(k, v, kind, axis, d).start())

    def await_pair(k, v, kind, arrival):
        axis, ghost = axes[kind], (pitch_ghost, span_ghost, axial_ghost)[kind]

        def one(held, d):
            copy = remote(held, held, k, v, kind, axis, d)
            if arrival:
                copy.wait_recv()
            else:
                copy.wait_send()

        if axis == "pitch":
            one(ghost.at[k, :, v], 0)
        else:
            pl.when(both[axis])(lambda: one(ghost.at[k, :, v], 0))
            for d in range(2):
                alone = jnp.logical_not(has[axis, 1 - d])
                pl.when(alone)(lambda: one(ghost.at[k, d, v], d))

    def pack_span(k, v):
        for i in range(NT):
            at = pl.ds(i * PC, PC)
            span_send[k, 0, v, at, :] = field[k, v, i, pl.ds(0, PC, CS), :]
            span_send[k, 1, v, at, :] = field[k, v, i, pl.ds(CS - 1, PC, CS), :]

    def split(values):
        high = values.astype(jnp.bfloat16)
        low = (values - high.astype(jnp.float32)).astype(jnp.bfloat16)
        return high, low

    def pack_axial(k, v, columns):
        tiles = columns.reshape(NT, PC, CS, CA)
        packed = tiles[0]
        for i in range(1, NT):
            packed = jnp.where(slot4 == i * PC, tiles[i], packed)
        tile = packed[0]
        for p in range(1, PC):
            tile = jnp.where(lax.bitwise_and(lane2, 3) == p, packed[p], tile)
        axial_send[k, v] = tile

    def shifted(k, v, columns):
        if columns.start:
            halves[v] = jnp.concatenate(split(field[k, v].reshape(NT * ROWS, CA)), axis=1)
        return jnp.dot(halves[v], shift[:, columns], preferred_element_type=jnp.float32)

    pl.semaphore_wait(barrier, 2 + sum(there.astype(jnp.int32) for there in has.values()))

    def send_faces(v, carry):
        start(0, v, 0)
        return carry

    lax.fori_loop(0, NVAR, send_faces, 0)

    source_lane = lax.bitwise_and(lax.broadcasted_iota(jnp.int32, (2 * CA, 2 * CA), 0), CA - 1)
    result_lane = lax.broadcasted_iota(jnp.int32, (2 * CA, 2 * CA), 1)
    adjacent = jnp.abs(source_lane - result_lane) == 1
    spread = source_lane == jnp.where(result_lane < CA + 64, CA - 1, 0)
    shift[...] = jnp.where(
        result_lane < CA, jnp.where(adjacent, 1.0, 0.0), jnp.where(spread, 1.0, 0.0)
    ).astype(jnp.bfloat16)
    source_lane = source_lane[:, :CA]
    result_lane = result_lane[:, :CA]
    inject[...] = jnp.where(
        result_lane == jnp.where(source_lane < 64, 0, CA - 1), 1.0, 0.0
    ).astype(jnp.bfloat16)
    tile_of = lax.broadcasted_iota(jnp.int32, (NT * PC, CS, CA), 0)
    lane_of = lax.broadcasted_iota(jnp.int32, (NT * PC, CS, CA), 2)
    mask[...] = (
        jnp.where(tile_of == lax.bitwise_and(lane_of, 63), 1.0, 0.0)
        .reshape(NT * ROWS, CA)
        .astype(jnp.bfloat16)
        .reshape(NT * PC // 2, 2 * CS, CA)
    )

    loads[0].wait()

    def pack_state(v, carry):
        pack_axial(0, v, shifted(0, v, slice(CA, 2 * CA)))
        start(0, v, 2)
        pack_span(0, v)
        start(0, v, 1)
        return carry

    lax.fori_loop(0, NVAR, pack_state, 0)

    for axis, ghost in (("span", span_ghost), ("axial", axial_ghost)):
        for d in range(2):

            @pl.when(jnp.logical_not(has[axis, d]))
            def _():
                def clear(v, carry):
                    for k in range(ROUNDS):
                        ghost[k, d, v] = jnp.zeros(ghost.shape[3:], jnp.float32)
                    return carry

                lax.fori_loop(0, NVAR, clear, 0)

    loads[1].wait()
    radius = [jnp.abs(velocity[d]) + 2.0 * VISCOSITY for d in range(3)]
    scale = CFL_RATIO / (radius[0] + radius[1] + radius[2])
    smoothing = []
    for d in range(3):
        ratio = radius[d] * scale
        smoothing.append(0.25 * jnp.maximum(ratio * ratio - 1.0, 0.0))
    inverse_diagonal = 1.0 / (1.0 + 2.0 * (smoothing[0] + smoothing[1] + smoothing[2]))
    centre = jnp.full(CELLS, -6.0 * VISCOSITY, jnp.float32)
    lower, upper = [], []
    for d in range(3):
        speed = velocity[d]
        lower.append(jnp.maximum(speed, 0.0) + VISCOSITY)
        upper.append(VISCOSITY - jnp.minimum(speed, 0.0))
        centre = centre - jnp.abs(speed)
    smooth = [smoothing[d] * inverse_diagonal for d in range(3)]
    on_top, on_bottom = row4 == CS - 1, row4 == 0
    for held, low, high in ((coef, lower, upper), (weight, smooth, smooth)):
        held[0] = low[0]
        held[1] = high[0]
        held[2] = jnp.where(on_bottom, 0.0, low[1])
        held[3] = jnp.where(on_top, 0.0, high[1])
        held[4] = jnp.where(on_bottom, low[1], 0.0)
        held[5] = jnp.where(on_top, high[1], 0.0)
        held[6] = jnp.where(lane == 0, low[2], high[2])
    weight[7] = inverse_diagonal
    weight[8] = smooth[2]
    coef[7] = centre
    coef[8] = jnp.where(lane == 0, 0.0, lower[2])
    coef[9] = jnp.where(lane == CA - 1, 0.0, upper[2])

    for load in loads[2:]:
        load.wait()
    rates = [
        rotor_ref[0] * (0.5 * (1 - 2 * (n % 2)) / math.sin(math.pi * n / NT))
        for n in range(1, HALF + 1)
    ]

    zero = jnp.zeros((1, CS, CA), jnp.float32)

    def inside(held, x):
        below = jnp.concatenate([zero, x[: PC - 1]], axis=0)
        above = jnp.concatenate([x[1:], zero], axis=0)
        return (
            held[0] * below
            + held[1] * above
            + held[2] * pltpu.roll(x, 1, 1)
            + held[3] * pltpu.roll(x, CS - 1, 1)
        )

    def local_part(v, carry):
        x = [cells(field[0, v, i]) for i in range(NT)]
        for i in range(NT):
            total = cells(forcing[v, i]) + coef[7] * x[i] + inside(coef, x[i])
            total = total + coef[8] * pltpu.roll(x[i], 1, 2)
            total = total + coef[9] * pltpu.roll(x[i], CA - 1, 2)
            for n in range(1, HALF + 1):
                total = total - rates[n - 1] * (x[(i - n) % NT] - x[(i + n) % NT])
            for w in range(NVAR):
                total = total - coupling_ref[v, w] * cells(field[0, w, i])
            partial[v, i] = flat(total)
        return carry

    lax.fori_loop(0, NVAR, local_part, 0)

    @pl.when(jnp.logical_or(on_first, on_last))
    def _():
        angle = jnp.full((CS, CA), rotor_ref[1], jnp.float32)
        c1 = jnp.cos(angle)
        s1 = jnp.sin(angle) * jnp.where(on_first, 1.0, -1.0)
        c2, s2 = c1 * c1 - s1 * s1, 2.0 * s1 * c1
        c3, s3 = c2 * c1 - s2 * s1, s2 * c1 + c2 * s1
        c4, s4 = c2 * c2 - s2 * s2, 2.0 * s2 * c2
        for n in range(NT):
            total = jnp.full((CS, CA), 1.0 / NT, jnp.float32)
            for h, (c, s) in enumerate(((c1, s1), (c2, s2), (c3, s3), (c4, s4)), 1):
                theta = h * 2.0 * math.pi * n / NT
                total = total + (2.0 / NT * math.cos(theta)) * c - (2.0 / NT * math.sin(theta)) * s
            table[n] = total
        forward = map_ref[...]
        pick[0] = lax.shift_right_logical(forward, 7)
        pick[1] = lax.bitwise_and(forward, CA - 1)

    @pl.when(on_last)
    def _():
        rows, cols = pick[0], pick[1]
        column = lax.broadcasted_iota(jnp.int32, (CA, CA), 0)
        total = jnp.zeros((2 * CS, CA), jnp.float32)
        for s in range(CS):
            hit = rows[s : s + 1, :] == row
            left = jnp.concatenate(
                [
                    jnp.where(hit, float(s), 0.0),
                    jnp.where(hit, lane2.astype(jnp.float32), 0.0),
                ],
                axis=0,
            )
            right = jnp.where(cols[s : s + 1, :] == column, 1.0, 0.0)
            total = total + lax.dot_general(
                left, right, (((1,), (1,)), ((), ())), preferred_element_type=jnp.float32
            )
        pick[0] = total[:CS].astype(jnp.int32)
        pick[1] = total[CS:].astype(jnp.int32)

    def map_face(k, v):
        slot = jnp.where(on_first, 0, 1)

        @pl.when(jnp.logical_or(on_first, on_last))
        def _():
            rows, cols = pick[0], pick[1]
            picked = []
            for i in range(NT):
                for s in range(CS):
                    line = pitch_ghost[k, slot, v, i, pl.ds(s, 1), :]
                    taken = jnp.take_along_axis(
                        jnp.broadcast_to(line, (CS, CA)), cols, axis=1, mode="promise_in_bounds"
                    )
                    total = jnp.where(rows == s, taken, total) if s else taken
                picked.append(total)
            for i in range(NT):
                total = table[0] * picked[i]
                for n in range(1, NT):
                    total = total + table[n] * picked[(i - n) % NT]
                pitch_ghost[k, slot, v, i] = total

    def injected(k, v):
        tile = jnp.where(lane2 < 64, axial_ghost[k, 0, v], axial_ghost[k, 1, v])
        left = [
            (part[None] * mask[...]).reshape(NT * ROWS, CA)
            for part in split(jnp.concatenate([tile, tile], axis=0))
        ]
        ends = jnp.dot(
            jnp.concatenate(left, axis=1), inject[...], preferred_element_type=jnp.float32
        )
        return ends.reshape(NT, PC, CS, CA)

    def step(k, v, carry):
        held = coef if k == 0 else weight
        last = k == ROUNDS - 1

        def complete(ends, i, p):
            at = pl.ds(i * PC + p, 1)
            rows = pl.ds(p * CS, CS)
            total = partial[v, i, rows] + held[6, p] * ends[i, p]
            total = total + held[4, p] * jnp.broadcast_to(span_ghost[k, 0, v, at, :], (CS, CA))
            total = total + held[5, p] * jnp.broadcast_to(span_ghost[k, 1, v, at, :], (CS, CA))
            if p == 0:
                total = total + held[0, p] * pitch_ghost[k, 0, v, i]
            if p == PC - 1:
                total = total + held[1, p] * pitch_ghost[k, 1, v, i]
            if k == 0:
                base[v, i, rows] = total * weight[7, p]
            if last:
                out_ref[v, i, rows] = total
            else:
                field[k + 1, v, i, rows] = total

        for kind in range(3):
            await_pair(k, v, kind, False)
        await_pair(k, v, 0, True)
        map_face(k, v)
        await_pair(k, v, 2, True)
        ends = injected(k, v)
        await_pair(k, v, 1, True)
        for i in range(NT):
            complete(ends, i, 0)
            complete(ends, i, PC - 1)
        if not last:
            start(k + 1, v, 0)
        for i in range(NT):
            for p in range(1, PC - 1):
                complete(ends, i, p)
        if last:
            return carry
        pack_axial(k + 1, v, shifted(k + 1, v, slice(CA, 2 * CA)))
        start(k + 1, v, 2)
        pack_span(k + 1, v)
        start(k + 1, v, 1)
        return carry

    def prepare(k, v, carry):
        around = shifted(k + 1, v, slice(0, CA)).reshape(NT, PC, CS, CA)
        for i in range(NT):
            x = cells(field[k + 1, v, i])
            total = cells(base[v, i]) + inside(weight, x) + weight[8] * around[i]
            partial[v, i] = flat(total)
        return carry

    for k in range(ROUNDS):
        lax.fori_loop(0, NVAR, functools.partial(step, k), 0)
        if k < ROUNDS - 1:
            lax.fori_loop(0, NVAR, functools.partial(prepare, k), 0)


def per_device(state, source, velocity, coupling, rotor, face_map):
    block = (NVAR, NT, ROWS, CA)
    anywhere = pl.BlockSpec(memory_space=pl.ANY)
    f32 = jnp.float32
    out = pl.pallas_call(
        kernel,
        out_shape=pltpu.VMEM(block, f32),
        in_specs=[anywhere] * 6,
        out_specs=pl.BlockSpec(memory_space=pltpu.VMEM),
        scratch_shapes=[
            pltpu.VMEM((ROUNDS,) + block, f32),
            pltpu.VMEM(block, f32),
            pltpu.VMEM(block, f32),
            pltpu.VMEM(block, f32),
            pltpu.VMEM((3,) + CELLS, f32),
            pltpu.VMEM((10,) + CELLS, f32),
            pltpu.VMEM((9,) + CELLS, f32),
            pltpu.VMEM((NT, CS, CA), f32),
            pltpu.VMEM((2, CS, CA), jnp.int32),
            pltpu.VMEM((NVAR, NT * ROWS, 2 * CA), jnp.bfloat16),
            pltpu.VMEM((2 * CA, 2 * CA), jnp.bfloat16),
            pltpu.VMEM((2 * CA, CA), jnp.bfloat16),
            pltpu.VMEM((NT * PC // 2, 2 * CS, CA), jnp.bfloat16),
            pltpu.VMEM((ROUNDS, 2, NVAR, NT, CS, CA), f32),
            pltpu.VMEM((ROUNDS, 2, NVAR, NT * PC, CA), f32),
            pltpu.VMEM((ROUNDS, 2, NVAR, NT * PC, CA), f32),
            pltpu.VMEM((ROUNDS, NVAR, CS, CA), f32),
            pltpu.VMEM((ROUNDS, 2, NVAR, CS, CA), f32),
            pltpu.SMEM((NVAR, NVAR), f32),
            pltpu.SMEM((2,), f32),
            pltpu.VMEM((CS, CA), jnp.int32),
            pltpu.SemaphoreType.DMA((6,)),
            pltpu.SemaphoreType.DMA((NVAR, 3)),
            pltpu.SemaphoreType.DMA((2, NVAR, 3)),
        ],
        compiler_params=pltpu.CompilerParams(
            collective_id=0, has_side_effects=True, vmem_limit_bytes=60 * 1024 * 1024
        ),
        cost_estimate=pl.CostEstimate(flops=20_000_000, bytes_accessed=2_300_000, transcendentals=0),
    )(state.reshape(block), source.reshape(block), velocity, coupling, rotor, face_map)
    return out.reshape(state.shape)


def solution(mesh):
    return jax.shard_map(
        per_device,
        mesh=mesh,
        in_specs=(
            P(None, None, "pitch", "span", "axial"),
            P(None, None, "pitch", "span", "axial"),
            P(None, "pitch", "span", "axial"),
            P(),
            P(),
            P("span", "axial"),
        ),
        out_specs=P(None, None, "pitch", "span", "axial"),
        check_vma=False,
    )
```

```python
import functools
import math

import jax
import jax.numpy as jnp
from jax import lax
from jax.experimental import pallas as pl
from jax.experimental.pallas import tpu as pltpu
from jax.sharding import PartitionSpec as P

NVAR = 5
NT = 9
PC = 4
CS = 8
CA = 128
ROWS = PC * CS
CELLS = (PC, CS, CA)
SWEEPS = 3
ROUNDS = SWEEPS + 1
VISCOSITY = 0.1
CFL_RATIO = 3.0
MESH = pl.DeviceIdType.MESH
HALF = (NT - 1) // 2


def cells(rows):
    return rows.reshape(CELLS)


def flat(values):
    return values.reshape(ROWS, CA)


def kernel(
    state_ref, source_ref, velocity_ref, coupling_in, rotor_in, map_in,
    out_ref,
    field, partial, base, forcing, velocity, coef, weight, table, pick,
    halves, shift, inject, mask,
    pitch_ghost, span_send, span_ghost, axial_send, axial_ghost,
    coupling_ref, rotor_ref, map_ref,
    load_sem, send_sem, recv_sem,
):
    place = {a: lax.axis_index(a) for a in ("pitch", "span", "axial")}
    count = {a: lax.axis_size(a) for a in ("pitch", "span", "axial")}
    axes = ("pitch", "span", "axial")
    has = {(a, 0): place[a] > 0 for a in axes[1:]}
    has.update({(a, 1): place[a] < count[a] - 1 for a in axes[1:]})
    both = {a: jnp.logical_and(has[a, 0], has[a, 1]) for a in axes[1:]}
    target = {(a, d): place[a] + 2 * d - 1 for a in axes[1:] for d in range(2)}
    target["pitch", 0] = lax.rem(place["pitch"] + count["pitch"] - 1, count["pitch"])
    target["pitch", 1] = lax.rem(place["pitch"] + 1, count["pitch"])
    on_first = place["pitch"] == 0
    on_last = place["pitch"] == count["pitch"] - 1

    def guarded(axis, d, action):
        if axis == "pitch":
            action()
        else:
            pl.when(has[axis, d])(action)

    barrier = pltpu.get_barrier_semaphore()
    for axis in axes:
        for d in range(2):

            def greet():
                pl.semaphore_signal(
                    barrier, inc=1, device_id={axis: target[axis, d]}, device_id_type=MESH
                )

            guarded(axis, d, greet)

    loads = [
        pltpu.make_async_copy(src, dst, load_sem.at[n])
        for n, (src, dst) in enumerate(
            (
                (state_ref, field.at[0]),
                (velocity_ref, velocity),
                (source_ref, forcing),
                (coupling_in, coupling_ref),
                (rotor_in, rotor_ref),
                (map_in, map_ref),
            )
        )
    ]
    for load in loads:
        load.start()

    lane = lax.broadcasted_iota(jnp.int32, CELLS, 2)
    row = lax.broadcasted_iota(jnp.int32, (CS, CA), 0)
    lane2 = lax.broadcasted_iota(jnp.int32, (CS, CA), 1)
    row4 = lax.broadcasted_iota(jnp.int32, CELLS, 1)
    slot4 = lax.bitwise_and(lane, 63) - lax.broadcasted_iota(jnp.int32, CELLS, 0)

    def remote(src, dst, k, v, kind, axis, d):
        return pltpu.make_async_remote_copy(
            src_ref=src,
            dst_ref=dst,
            send_sem=send_sem.at[v, kind],
            recv_sem=recv_sem.at[k % 2, v, kind],
            device_id={axis: target[axis, d]},
            device_id_type=MESH,
        )

    def transfers(k, v, kind, axis, d):
        if axis == "pitch":
            faces = state_ref if k == 0 else field.at[k]
            src = faces.at[v, :, pl.ds((ROWS - CS) * d, CS)]
            ghost = pitch_ghost
        elif axis == "span":
            src, ghost = span_send.at[k, d, v], span_ghost
        else:
            src, ghost = axial_send.at[k, v], axial_ghost
        return remote(src, ghost.at[k, 1 - d, v], k, v, kind, axis, d)

    def start(k, v, kind):
        axis = axes[kind]
        for d in range(2):
            guarded(axis, d, lambda: transfers(k, v, kind, axis, d).start())

    def await_pair(k, v, kind, arrival):
        axis, ghost = axes[kind], (pitch_ghost, span_ghost, axial_ghost)[kind]

        def one(held, d):
            copy = remote(held, held, k, v, kind, axis, d)
            if arrival:
                copy.wait_recv()
            else:
                copy.wait_send()

        if axis == "pitch":
            one(ghost.at[k, :, v], 0)
        else:
            pl.when(both[axis])(lambda: one(ghost.at[k, :, v], 0))
            for d in range(2):
                alone = jnp.logical_not(has[axis, 1 - d])
                pl.when(alone)(lambda: one(ghost.at[k, d, v], d))

    def pack_span(k, v):
        for i in range(NT):
            at = pl.ds(i * PC, PC)
            span_send[k, 0, v, at, :] = field[k, v, i, pl.ds(0, PC, CS), :]
            span_send[k, 1, v, at, :] = field[k, v, i, pl.ds(CS - 1, PC, CS), :]

    def split(values):
        high = values.astype(jnp.bfloat16)
        low = (values - high.astype(jnp.float32)).astype(jnp.bfloat16)
        return high, low

    def pack_axial(k, v, columns):
        tiles = columns.reshape(NT, PC, CS, CA)
        packed = tiles[0]
        for i in range(1, NT):
            packed = jnp.where(slot4 == i * PC, tiles[i], packed)
        tile = packed[0]
        for p in range(1, PC):
            tile = jnp.where(lax.bitwise_and(lane2, 3) == p, packed[p], tile)
        axial_send[k, v] = tile

    def shifted(k, v, columns):
        if columns.start:
            halves[v] = jnp.concatenate(split(field[k, v].reshape(NT * ROWS, CA)), axis=1)
        return jnp.dot(halves[v], shift[:, columns], preferred_element_type=jnp.float32)

    pl.semaphore_wait(barrier, 2 + sum(there.astype(jnp.int32) for there in has.values()))

    def send_faces(v, carry):
        start(0, v, 0)
        return carry

    lax.fori_loop(0, NVAR, send_faces, 0)

    source_lane = lax.bitwise_and(lax.broadcasted_iota(jnp.int32, (2 * CA, 2 * CA), 0), CA - 1)
    result_lane = lax.broadcasted_iota(jnp.int32, (2 * CA, 2 * CA), 1)
    adjacent = jnp.abs(source_lane - result_lane) == 1
    spread = source_lane == jnp.where(result_lane < CA + 64, CA - 1, 0)
    shift[...] = jnp.where(
        result_lane < CA, jnp.where(adjacent, 1.0, 0.0), jnp.where(spread, 1.0, 0.0)
    ).astype(jnp.bfloat16)
    source_lane = source_lane[:, :CA]
    result_lane = result_lane[:, :CA]
    inject[...] = jnp.where(
        result_lane == jnp.where(source_lane < 64, 0, CA - 1), 1.0, 0.0
    ).astype(jnp.bfloat16)
    tile_of = lax.broadcasted_iota(jnp.int32, (NT * PC, CS, CA), 0)
    lane_of = lax.broadcasted_iota(jnp.int32, (NT * PC, CS, CA), 2)
    mask[...] = (
        jnp.where(tile_of == lax.bitwise_and(lane_of, 63), 1.0, 0.0)
        .reshape(NT * ROWS, CA)
        .astype(jnp.bfloat16)
        .reshape(NT * PC // 2, 2 * CS, CA)
    )

    loads[0].wait()

    def pack_state(v, carry):
        pack_axial(0, v, shifted(0, v, slice(CA, 2 * CA)))
        start(0, v, 2)
        pack_span(0, v)
        start(0, v, 1)
        return carry

    lax.fori_loop(0, NVAR, pack_state, 0)

    for axis, ghost in (("span", span_ghost), ("axial", axial_ghost)):
        for d in range(2):

            @pl.when(jnp.logical_not(has[axis, d]))
            def _():
                def clear(v, carry):
                    for k in range(ROUNDS):
                        ghost[k, d, v] = jnp.zeros(ghost.shape[3:], jnp.float32)
                    return carry

                lax.fori_loop(0, NVAR, clear, 0)

    loads[1].wait()
    radius = [jnp.abs(velocity[d]) + 2.0 * VISCOSITY for d in range(3)]
    scale = CFL_RATIO / (radius[0] + radius[1] + radius[2])
    smoothing = []
    for d in range(3):
        ratio = radius[d] * scale
        smoothing.append(0.25 * jnp.maximum(ratio * ratio - 1.0, 0.0))
    inverse_diagonal = 1.0 / (1.0 + 2.0 * (smoothing[0] + smoothing[1] + smoothing[2]))
    centre = jnp.full(CELLS, -6.0 * VISCOSITY, jnp.float32)
    lower, upper = [], []
    for d in range(3):
        speed = velocity[d]
        lower.append(jnp.maximum(speed, 0.0) + VISCOSITY)
        upper.append(VISCOSITY - jnp.minimum(speed, 0.0))
        centre = centre - jnp.abs(speed)
    smooth = [smoothing[d] * inverse_diagonal for d in range(3)]
    on_top, on_bottom = row4 == CS - 1, row4 == 0
    for held, low, high in ((coef, lower, upper), (weight, smooth, smooth)):
        held[0] = low[0]
        held[1] = high[0]
        held[2] = jnp.where(on_bottom, 0.0, low[1])
        held[3] = jnp.where(on_top, 0.0, high[1])
        held[4] = jnp.where(on_bottom, low[1], 0.0)
        held[5] = jnp.where(on_top, high[1], 0.0)
        held[6] = jnp.where(lane == 0, low[2], high[2])
    weight[7] = inverse_diagonal
    weight[8] = smooth[2]
    coef[7] = centre
    coef[8] = jnp.where(lane == 0, 0.0, lower[2])
    coef[9] = jnp.where(lane == CA - 1, 0.0, upper[2])

    for load in loads[2:]:
        load.wait()
    rates = [
        rotor_ref[0] * (0.5 * (1 - 2 * (n % 2)) / math.sin(math.pi * n / NT))
        for n in range(1, HALF + 1)
    ]

    zero = jnp.zeros((1, CS, CA), jnp.float32)

    def inside(held, x):
        below = jnp.concatenate([zero, x[: PC - 1]], axis=0)
        above = jnp.concatenate([x[1:], zero], axis=0)
        return (
            held[0] * below
            + held[1] * above
            + held[2] * pltpu.roll(x, 1, 1)
            + held[3] * pltpu.roll(x, CS - 1, 1)
        )

    def local_part(v, carry):
        x = [cells(field[0, v, i]) for i in range(NT)]
        for i in range(NT):
            total = cells(forcing[v, i]) + coef[7] * x[i] + inside(coef, x[i])
            total = total + coef[8] * pltpu.roll(x[i], 1, 2)
            total = total + coef[9] * pltpu.roll(x[i], CA - 1, 2)
            for n in range(1, HALF + 1):
                total = total - rates[n - 1] * (x[(i - n) % NT] - x[(i + n) % NT])
            for w in range(NVAR):
                total = total - coupling_ref[v, w] * cells(field[0, w, i])
            partial[v, i] = flat(total)
        return carry

    lax.fori_loop(0, NVAR, local_part, 0)

    @pl.when(jnp.logical_or(on_first, on_last))
    def _():
        angle = jnp.full((CS, CA), rotor_ref[1], jnp.float32)
        c1 = jnp.cos(angle)
        s1 = jnp.sin(angle) * jnp.where(on_first, 1.0, -1.0)
        c2, s2 = c1 * c1 - s1 * s1, 2.0 * s1 * c1
        c3, s3 = c2 * c1 - s2 * s1, s2 * c1 + c2 * s1
        c4, s4 = c2 * c2 - s2 * s2, 2.0 * s2 * c2
        for n in range(NT):
            total = jnp.full((CS, CA), 1.0 / NT, jnp.float32)
            for h, (c, s) in enumerate(((c1, s1), (c2, s2), (c3, s3), (c4, s4)), 1):
                theta = h * 2.0 * math.pi * n / NT
                total = total + (2.0 / NT * math.cos(theta)) * c - (2.0 / NT * math.sin(theta)) * s
            table[n] = total
        forward = map_ref[...]
        pick[0] = lax.shift_right_logical(forward, 7)
        pick[1] = lax.bitwise_and(forward, CA - 1)

    @pl.when(on_last)
    def _():
        rows, cols = pick[0], pick[1]
        column = lax.broadcasted_iota(jnp.int32, (CA, CA), 0)
        total = jnp.zeros((2 * CS, CA), jnp.float32)
        for s in range(CS):
            hit = rows[s : s + 1, :] == row
            left = jnp.concatenate(
                [
                    jnp.where(hit, float(s), 0.0),
                    jnp.where(hit, lane2.astype(jnp.float32), 0.0),
                ],
                axis=0,
            )
            right = jnp.where(cols[s : s + 1, :] == column, 1.0, 0.0)
            total = total + lax.dot_general(
                left, right, (((1,), (1,)), ((), ())), preferred_element_type=jnp.float32
            )
        pick[0] = total[:CS].astype(jnp.int32)
        pick[1] = total[CS:].astype(jnp.int32)

    def map_face(k, v):
        slot = jnp.where(on_first, 0, 1)

        @pl.when(jnp.logical_or(on_first, on_last))
        def _():
            rows, cols = pick[0], pick[1]
            picked = []
            for i in range(NT):
                for s in range(CS):
                    line = pitch_ghost[k, slot, v, i, pl.ds(s, 1), :]
                    taken = jnp.take_along_axis(
                        jnp.broadcast_to(line, (CS, CA)), cols, axis=1, mode="promise_in_bounds"
                    )
                    total = jnp.where(rows == s, taken, total) if s else taken
                picked.append(total)
            for i in range(NT):
                total = table[0] * picked[i]
                for n in range(1, NT):
                    total = total + table[n] * picked[(i - n) % NT]
                pitch_ghost[k, slot, v, i] = total

    def injected(k, v):
        tile = jnp.where(lane2 < 64, axial_ghost[k, 0, v], axial_ghost[k, 1, v])
        left = [
            (part[None] * mask[...]).reshape(NT * ROWS, CA)
            for part in split(jnp.concatenate([tile, tile], axis=0))
        ]
        ends = jnp.dot(
            jnp.concatenate(left, axis=1), inject[...], preferred_element_type=jnp.float32
        )
        return ends.reshape(NT, PC, CS, CA)

    def step(k, v, carry):
        held = coef if k == 0 else weight
        last = k == ROUNDS - 1

        def put(i, p, total):
            rows = pl.ds(p * CS, CS)
            if k == 0:
                base[v, i, rows] = total * weight[7, p]
            if last:
                out_ref[v, i, rows] = total
            else:
                field[k + 1, v, i, rows] = total

        for kind in range(3):
            await_pair(k, v, kind, False)
        await_pair(k, v, 2, True)
        ends = injected(k, v)
        await_pair(k, v, 1, True)
        for i in range(NT):
            for p in range(PC):
                at = pl.ds(i * PC + p, 1)
                rows = pl.ds(p * CS, CS)
                total = partial[v, i, rows] + held[6, p] * ends[i, p]
                total = total + held[4, p] * jnp.broadcast_to(span_ghost[k, 0, v, at, :], (CS, CA))
                total = total + held[5, p] * jnp.broadcast_to(span_ghost[k, 1, v, at, :], (CS, CA))
                if 0 < p < PC - 1:
                    put(i, p, total)
                else:
                    partial[v, i, rows] = total
        await_pair(k, v, 0, True)
        map_face(k, v)
        for i in range(NT):
            for d, p in ((0, 0), (1, PC - 1)):
                face = held[d, p] * pitch_ghost[k, d, v, i]
                put(i, p, partial[v, i, pl.ds(p * CS, CS)] + face)
        if last:
            return carry
        start(k + 1, v, 0)
        pack_axial(k + 1, v, shifted(k + 1, v, slice(CA, 2 * CA)))
        start(k + 1, v, 2)
        pack_span(k + 1, v)
        start(k + 1, v, 1)
        return carry

    def prepare(k, v, carry):
        around = shifted(k + 1, v, slice(0, CA)).reshape(NT, PC, CS, CA)
        for i in range(NT):
            x = cells(field[k + 1, v, i])
            total = cells(base[v, i]) + inside(weight, x) + weight[8] * around[i]
            partial[v, i] = flat(total)
        return carry

    for k in range(ROUNDS):
        lax.fori_loop(0, NVAR, functools.partial(step, k), 0)
        if k < ROUNDS - 1:
            lax.fori_loop(0, NVAR, functools.partial(prepare, k), 0)


def per_device(state, source, velocity, coupling, rotor, face_map):
    block = (NVAR, NT, ROWS, CA)
    anywhere = pl.BlockSpec(memory_space=pl.ANY)
    f32 = jnp.float32
    out = pl.pallas_call(
        kernel,
        out_shape=pltpu.VMEM(block, f32),
        in_specs=[anywhere] * 6,
        out_specs=pl.BlockSpec(memory_space=pltpu.VMEM),
        scratch_shapes=[
            pltpu.VMEM((ROUNDS,) + block, f32),
            pltpu.VMEM(block, f32),
            pltpu.VMEM(block, f32),
            pltpu.VMEM(block, f32),
            pltpu.VMEM((3,) + CELLS, f32),
            pltpu.VMEM((10,) + CELLS, f32),
            pltpu.VMEM((9,) + CELLS, f32),
            pltpu.VMEM((NT, CS, CA), f32),
            pltpu.VMEM((2, CS, CA), jnp.int32),
            pltpu.VMEM((NVAR, NT * ROWS, 2 * CA), jnp.bfloat16),
            pltpu.VMEM((2 * CA, 2 * CA), jnp.bfloat16),
            pltpu.VMEM((2 * CA, CA), jnp.bfloat16),
            pltpu.VMEM((NT * PC // 2, 2 * CS, CA), jnp.bfloat16),
            pltpu.VMEM((ROUNDS, 2, NVAR, NT, CS, CA), f32),
            pltpu.VMEM((ROUNDS, 2, NVAR, NT * PC, CA), f32),
            pltpu.VMEM((ROUNDS, 2, NVAR, NT * PC, CA), f32),
            pltpu.VMEM((ROUNDS, NVAR, CS, CA), f32),
            pltpu.VMEM((ROUNDS, 2, NVAR, CS, CA), f32),
            pltpu.SMEM((NVAR, NVAR), f32),
            pltpu.SMEM((2,), f32),
            pltpu.VMEM((CS, CA), jnp.int32),
            pltpu.SemaphoreType.DMA((6,)),
            pltpu.SemaphoreType.DMA((NVAR, 3)),
            pltpu.SemaphoreType.DMA((2, NVAR, 3)),
        ],
        compiler_params=pltpu.CompilerParams(
            collective_id=0, has_side_effects=True, vmem_limit_bytes=60 * 1024 * 1024
        ),
        cost_estimate=pl.CostEstimate(flops=20_000_000, bytes_accessed=2_300_000, transcendentals=0),
    )(state.reshape(block), source.reshape(block), velocity, coupling, rotor, face_map)
    return out.reshape(state.shape)


def solution(mesh):
    return jax.shard_map(
        per_device,
        mesh=mesh,
        in_specs=(
            P(None, None, "pitch", "span", "axial"),
            P(None, None, "pitch", "span", "axial"),
            P(None, "pitch", "span", "axial"),
            P(),
            P(),
            P("span", "axial"),
        ),
        out_specs=P(None, None, "pitch", "span", "axial"),
        check_vma=False,
    )
```
